32 devices in a mesh: lev: 2 (over x), hor: 16 (over z, y, core).
Axes of the slice: x: 2, y: 2, z: 4, core: 2. Of those that a mesh axis runs over, the one named last changes fastest.
Arguments:
- slab_fields: float32 [4, 32, 65536], P(None, 'lev', 'hor'), may hold values from -6 to 6
- sample_index: int32 [16, 256], P('hor', 'lev'), may hold values from 0 to 2047
- thickness: float32 [32], replicated, may hold values from 0.3 to 3
- level_cuts: int32 [31], replicated, may hold values 0 or 1
Outputs:
- gram: float32 [2176, 2176], P('hor', 'lev')
The draws below stay inside these ranges and needn't reach their ends.
Inputs may be any that keep to these rules, and one draw needn't show every extreme that they name: sample_index[j, k] indexes a column among the 2048 columns that start at j * 4096 + (k // 128) * 2048.
All inputs are finite; a program needn't handle non-finite values.
Results may differ from the reference program's by a relative error of at most 0.00068.
Values may be sent and summed in bfloat16 or wider, within the bound.
A program may use at most 128 MiB of HBM per device.

```python
import math
import jax
import jax.numpy as jnp
from jax import lax

LEV = 32
CPD = 2048
SAMP = 128
F = 2176
BLOCK_COLS = 4096
COLS = 65536
SAMPLES_ALL = 4096
N_LEV = 2
N_HOR = 16


def place_ends(values, key, least, largest):
    place = [jax.random.randint(jax.random.fold_in(key, axis), (), 0, length) for axis, length in enumerate(values.shape)]
    longest = values.shape.index(max(values.shape))
    next_to = place[:longest] + [(place[longest] + 1) % values.shape[longest]] + place[longest + 1:]
    return values.at[tuple(place)].set(least).at[tuple(next_to)].set(largest)


def with_spikes(entries, own_key, source, target, parts, factor):
    owner, partner = [(jnp.arange(entries.shape[position]) // (entries.shape[position] // parts)).reshape([-1 if axis == position else 1 for axis in range(entries.ndim)]) for position in (source, target)]
    chosen = jax.random.permutation(own_key, parts)[partner]
    strong = (owner == chosen) | (owner == (partner + parts // 2) % parts)
    return jnp.where(strong, factor * entries, entries)


def level_of(own_key, dims, pieces, low, high):
    gain = 1.0
    for dim, blocks in pieces:
        draws = jax.random.uniform(jax.random.fold_in(jax.random.fold_in(own_key, 6), dim), (blocks,), jnp.float32, low / len(pieces), high / len(pieces))
        gain = gain * jnp.repeat(jnp.exp(draws), dims[dim] // blocks).reshape((-1,) + (1,) * (len(dims) - 1 - dim))
    return gain


def gaussian_with(own_key, shape, spread, reach, split, heavy, kind=jnp.bfloat16):
    entries = spread * jax.random.normal(own_key, shape, jnp.float32)
    if split:
        entries = entries * level_of(own_key, shape, split, -0.22, 0.18)
    return jnp.clip(with_spikes(entries, jax.random.fold_in(own_key, 3), *heavy), -reach, reach).astype(kind)


def setup_inputs(seed: int = 0) -> dict:
    streams_of = jax.random.split(jax.random.key(seed), 5)
    slab_fields = gaussian_with(streams_of[0], (4, LEV, COLS), 1.0, 6.0, ((1, 2), (2, 16)), (2, 1, 16, 2.0), jnp.float32)
    sample_index = place_ends(jax.random.randint(streams_of[1], (N_HOR, N_LEV * SAMP), 0, CPD), jax.random.fold_in(streams_of[1], 1), 0, CPD - 1).astype(jnp.int32)
    thickness = jnp.clip(jnp.exp(jax.random.uniform(streams_of[2], (LEV,), jnp.float32, math.log(0.3), math.log(3.0))), 0.3, 3.0)
    level_cuts = place_ends((jax.random.randint(streams_of[3], (LEV - 1,), 0, 4) < 1).astype(jnp.int32), jax.random.fold_in(streams_of[3], 1), 0, 1)
    return {"slab_fields": slab_fields, "sample_index": sample_index, "thickness": thickness, "level_cuts": level_cuts}


def vertical_filter(values, thickness, level_cuts):
    link = 1.0 - level_cuts.astype(jnp.float32)
    zero_one = jnp.zeros((1,), jnp.float32)
    lower_link = jnp.concatenate([zero_one, link])
    upper_link = jnp.concatenate([link, zero_one])
    lower_weight = jnp.concatenate([zero_one, thickness[:-1]]) * lower_link
    upper_weight = jnp.concatenate([thickness[1:], zero_one]) * upper_link
    zero_row = jnp.zeros_like(values[:, :1, :])
    below = jnp.concatenate([zero_row, values[:, :-1, :]], axis=1)
    above = jnp.concatenate([values[:, 1:, :], zero_row], axis=1)
    numer = 2.0 * thickness[None, :, None] * values + lower_weight[None, :, None] * below + upper_weight[None, :, None] * above
    denom = 2.0 * thickness + lower_weight + upper_weight
    return numer / denom[None, :, None]


def quadratic_features(smooth):
    count = smooth.shape[2]
    later = jnp.concatenate([smooth[2], smooth[3]], axis=0)
    earlier = jnp.concatenate([smooth[0], smooth[1]], axis=0)
    product = (later[:, None, :] * smooth[0][None, :, :]).reshape(-1, count)
    return jnp.concatenate([later, earlier, product], axis=0).astype(jnp.bfloat16)


def reference(slab_fields, sample_index, thickness, level_cuts):
    block_base = (jnp.arange(N_HOR) * BLOCK_COLS).astype(jnp.int32)
    group_base = ((jnp.arange(N_LEV * SAMP) // SAMP) * CPD).astype(jnp.int32)
    columns = (block_base[:, None] + group_base[None, :] + sample_index).astype(jnp.int32)

    def add_block(total, index_row):
        picked = jnp.take(slab_fields, index_row, axis=2)
        features = quadratic_features(vertical_filter(picked, thickness, level_cuts)).astype(jnp.float32)
        return total + jnp.dot(features, features.T, precision=lax.Precision.HIGHEST, preferred_element_type=jnp.float32), None

    start = jnp.zeros((F, F), jnp.float32)
    total, _ = lax.scan(add_block, start, columns)
    return total / SAMPLES_ALL
```

```python
import jax
import jax.numpy as jnp
from jax import lax
from jax.experimental import pallas as pl
from jax.experimental.pallas import tpu as pltpu
from jax.sharding import PartitionSpec as P

MESH = pl.DeviceIdType.MESH


def filter_weights(thickness, level_cuts):
    link = 1.0 - level_cuts.astype(jnp.float32)
    zero_one = jnp.zeros((1,), jnp.float32)
    lower_link = jnp.concatenate([zero_one, link])
    upper_link = jnp.concatenate([link, zero_one])
    lower_weight = jnp.concatenate([zero_one, thickness[:-1]]) * lower_link
    upper_weight = jnp.concatenate([thickness[1:], zero_one]) * upper_link
    return lower_weight, upper_weight


def vertical_filter(values, thickness, level_cuts):
    lower_weight, upper_weight = filter_weights(thickness, level_cuts)
    zero_row = jnp.zeros_like(values[:, :1, :])
    below = jnp.concatenate([zero_row, values[:, :-1, :]], axis=1)
    above = jnp.concatenate([values[:, 1:, :], zero_row], axis=1)
    numer = (
        2.0 * thickness[None, :, None] * values
        + lower_weight[None, :, None] * below
        + upper_weight[None, :, None] * above
    )
    denom = 2.0 * thickness + lower_weight + upper_weight
    return numer / denom[None, :, None]


def quadratic_features(smooth):
    count = smooth.shape[2]
    later = jnp.concatenate([smooth[2], smooth[3]], axis=0)
    earlier = jnp.concatenate([smooth[0], smooth[1]], axis=0)
    product = (later[:, None, :] * smooth[0][None, :, :]).reshape(-1, count)
    return jnp.concatenate([later, earlier, product], axis=0).astype(jnp.bfloat16)


def general_plan(slab_fields, sample_index, thickness, level_cuts):
    samp_count = sample_index.shape[1]
    lev_count = lax.axis_size("lev")
    hor_count = lax.axis_size("hor")
    all_lists = lax.all_gather(sample_index, "lev", axis=1, tiled=True)[0]
    group_cols = slab_fields.shape[2] // lev_count
    offsets = jnp.arange(all_lists.shape[0]) // samp_count * group_cols + all_lists
    chosen = jnp.take(slab_fields, offsets, axis=2)
    picked_cols = lax.all_to_all(chosen, "lev", split_axis=2, concat_axis=1, tiled=True)
    smooth = vertical_filter(picked_cols, thickness, level_cuts)
    feat_count = 4 * smooth.shape[1] + 2 * smooth.shape[1] * smooth.shape[1]
    col_count = feat_count // lev_count
    col_start = lax.axis_index("lev") * col_count
    features_bf = quadratic_features(smooth)
    block_features_bf = lax.all_gather(features_bf, "lev", axis=1, tiled=True)
    chosen_rows = lax.dynamic_slice_in_dim(block_features_bf, col_start, col_count, 0)
    column_block = lax.dot_general(
        block_features_bf, chosen_rows, (((1,), (1,)), ((), ())), preferred_element_type=jnp.float32
    )
    gram_block = lax.psum_scatter(column_block, "hor", scatter_dimension=0, tiled=True)
    count_all = samp_count * lev_count * hor_count
    return gram_block / count_all


def gram_kernel(
    slab_ref, idx_ref, coef_ref, out_ref,
    buf, other_idx, later_ref, rows_ref, cols_ref, recv_sem, send_sem, idx_sem,
):
    group_cols = slab_ref.shape[2] // 2
    x = lax.axis_index("lev")
    h = lax.axis_index("hor")
    z, y, c = h // 4, h // 2 % 2, h % 2

    def along_z(k):
        return (z // 2 + k // 2) % 2 * 2 + (z + k) % 2

    def place(zz, yy, cc):
        return zz * 4 + yy * 2 + cc

    def piece(xx, hh, g):
        return (xx * 16 + hh) * 2 + g

    x_mate = (1 - x, h)
    y_mate = (x, place(z, 1 - y, c))
    core_mate = (x, place(z, y, 1 - c))
    z_mates = [(x, place(along_z(k), y, c)) for k in (1, 2, 3)]

    def send(p, target):
        pltpu.make_async_remote_copy(
            src_ref=buf.at[p], dst_ref=buf.at[p], send_sem=send_sem, recv_sem=recv_sem.at[p],
            device_id=target, device_id_type=MESH,
        ).start()

    def arrive(p):
        pltpu.make_async_copy(buf.at[p], buf.at[p], recv_sem.at[p]).wait()

    barrier = pltpu.get_barrier_semaphore()
    for mate in [x_mate, y_mate, core_mate] + z_mates:
        pl.semaphore_signal(barrier, inc=1, device_id=mate, device_id_type=MESH)
    pl.semaphore_wait(barrier, 6)

    idx_copy = pltpu.make_async_remote_copy(
        src_ref=idx_ref, dst_ref=other_idx, send_sem=idx_sem.at[0], recv_sem=idx_sem.at[1],
        device_id=x_mate, device_id_type=MESH,
    )
    idx_copy.start()

    def pick(g, idx_row):
        step = 512
        total = jnp.zeros((192, 128), jnp.float32)
        for t in range(group_cols // step):
            start = pl.multiple_of(g * group_cols + t * step, step)
            v = slab_ref[:, :, pl.ds(start, step)].reshape(64, step)
            hi = v.astype(jnp.bfloat16)
            rest = v - hi.astype(jnp.float32)
            mid = rest.astype(jnp.bfloat16)
            low = (rest - mid.astype(jnp.float32)).astype(jnp.bfloat16)
            parts = jnp.concatenate([hi, mid, low], axis=0)
            lane = lax.broadcasted_iota(jnp.int32, (step, 128), 0) + t * step
            hot = jnp.where(lane == idx_row, 1.0, 0.0).astype(jnp.bfloat16)
            total += jnp.dot(parts, hot, preferred_element_type=jnp.float32)
        p = piece(x, h, g)
        buf[p] = total[0:64] + total[64:128] + total[128:192]
        for mate in z_mates + [x_mate, y_mate, core_mate]:
            send(p, mate)

    pick(x, idx_ref[...])
    idx_copy.wait_recv()
    pick(1 - x, other_idx[...])

    out_ref[...] = jnp.zeros_like(out_ref)

    def forward_z(i, carry):
        g = (x + i) % 2
        p = piece(x, place(along_z(1 + i // 2), y, c), g)
        arrive(p)
        for mate in [x_mate, y_mate, core_mate]:
            send(p, mate)
        return carry

    lax.fori_loop(0, 6, forward_z, 0)

    first_row = 136 * h - 128
    past_first = (h + 15) // 16
    first_row = first_row * past_first
    first_m = first_row // 32
    row_start = pl.multiple_of(past_first * (128 + first_row - 32 * first_m), 8)

    def add_block(hh):
        for g in range(2):
            lanes = slice(g * 128, g * 128 + 128)
            below_p, above_p = piece(0, hh, g), piece(1, hh, g)
            smooth = []
            for f in range(4):
                levels = slice(16 * f, 16 * f + 16)
                v = jnp.concatenate([buf[below_p, levels, :], buf[above_p, levels, :]], axis=0)
                smooth.append(
                    coef_ref[0] * v
                    + coef_ref[1] * pltpu.roll(v, 1, 0)
                    + coef_ref[2] * pltpu.roll(v, 31, 0)
                )
            later_ref[g, 0:32, :] = smooth[2]
            later_ref[g, 32:64, :] = smooth[3]
            rows_ref[0:32, lanes] = smooth[2]
            rows_ref[32:64, lanes] = smooth[3]
            rows_ref[64:96, lanes] = smooth[0]
            rows_ref[96:128, lanes] = smooth[1]
            base = smooth[0]
            for i in range(5):
                m_row = later_ref[g, pl.ds(first_m + i, 1), :]
                rows_ref[128 + 32 * i:160 + 32 * i, lanes] = m_row * base
            for b in range(4, 34):
                m_row = later_ref[g, pl.ds(b - 4 + 34 * x, 1), :]
                cols_ref[32 * b:32 * b + 32, lanes] = (m_row * base).astype(jnp.bfloat16)

            @pl.when(x == 0)
            def _():
                cols_ref[0:128, lanes] = rows_ref[0:128, lanes].astype(jnp.bfloat16)

            @pl.when(x == 1)
            def _():
                s0 = rows_ref[64:96, lanes]
                for b in range(4):
                    cols_ref[32 * b:32 * b + 32, lanes] = (later_ref[g, 30 + b:31 + b, :] * s0).astype(jnp.bfloat16)

        lhs = rows_ref[pl.ds(row_start, 136), :].astype(jnp.bfloat16)
        out_ref[...] += lax.dot_general(
            lhs, cols_ref[...], (((1,), (1,)), ((), ())), preferred_element_type=jnp.float32
        )

    def step(t, carry):
        zz = along_z(t % 4)
        far = t // 4
        near = place(zz, y, c)
        across = place(zz, 1 - y, c)

        @pl.when(far == 0)
        def _():
            p = piece(1 - x, near, 1)
            arrive(p)
            send(p, y_mate)
            send(p, core_mate)
            p = piece(x, across, 0)
            arrive(p)
            send(p, x_mate)
            send(p, core_mate)
            for p in (piece(1 - x, near, 0), piece(x, across, 1)):
                arrive(p)
                send(p, core_mate)

        @pl.when(far == 1)
        def _():
            for g in range(2):
                p = piece(1 - x, across, g)
                arrive(p)
                send(p, core_mate)

        yy = (y + far) % 2

        def one(i, inner):
            hh = place(zz, yy, (c + i) % 2)

            @pl.when(i == 1)
            def _():
                for xx in range(2):
                    for g in range(2):
                        arrive(piece(xx, hh, g))

            add_block(hh)
            return inner

        lax.fori_loop(0, 2, one, 0)
        return carry

    lax.fori_loop(0, 8, step, 0)
    out_ref[...] = out_ref[...] * (1.0 / 4096)
    sent = buf.at[pl.ds(0, 62)]
    pltpu.make_async_copy(sent, sent, send_sem).wait()
    idx_copy.wait_send()


def on_slice(slab_fields, sample_index, thickness, level_cuts):
    lower_weight, upper_weight = filter_weights(thickness, level_cuts)
    denom = 2.0 * thickness + lower_weight + upper_weight
    coef = jnp.stack([2.0 * thickness, lower_weight, upper_weight]) / denom
    coef = jnp.broadcast_to(coef[:, :, None], (3, 32, 128))
    vmem = pl.BlockSpec(memory_space=pltpu.VMEM)
    return pl.pallas_call(
        gram_kernel,
        out_shape=jax.ShapeDtypeStruct((136, 1088), jnp.float32),
        in_specs=[vmem] * 3,
        out_specs=vmem,
        scratch_shapes=[
            pltpu.VMEM((64, 64, 128), jnp.float32),
            pltpu.VMEM((1, 128), jnp.int32),
            pltpu.VMEM((2, 64, 128), jnp.float32),
            pltpu.VMEM((288, 256), jnp.float32),
            pltpu.VMEM((1088, 256), jnp.bfloat16),
            pltpu.SemaphoreType.DMA((64,)),
            pltpu.SemaphoreType.DMA,
            pltpu.SemaphoreType.DMA((2,)),
        ],
        compiler_params=pltpu.CompilerParams(
            collective_id=0, has_side_effects=True, vmem_limit_bytes=32 * 1024 * 1024
        ),
    )(slab_fields, sample_index, coef)


def solution(mesh):
    in_specs = (P(None, "lev", "hor"), P("hor", "lev"), P(), P())
    out_specs = P("hor", "lev")
    small = mesh.shape["lev"] == 2 and mesh.shape["hor"] == 16
    return jax.shard_map(
        on_slice if small else general_plan,
        mesh=mesh, in_specs=in_specs, out_specs=out_specs, check_vma=False,
    )
```

```python
import jax
import jax.numpy as jnp
from jax import lax
from jax.experimental import pallas as pl
from jax.experimental.pallas import tpu as pltpu
from jax.sharding import PartitionSpec as P

MESH = pl.DeviceIdType.MESH


def filter_weights(thickness, level_cuts):
    link = 1.0 - level_cuts.astype(jnp.float32)
    zero_one = jnp.zeros((1,), jnp.float32)
    lower_link = jnp.concatenate([zero_one, link])
    upper_link = jnp.concatenate([link, zero_one])
    lower_weight = jnp.concatenate([zero_one, thickness[:-1]]) * lower_link
    upper_weight = jnp.concatenate([thickness[1:], zero_one]) * upper_link
    return lower_weight, upper_weight


def vertical_filter(values, thickness, level_cuts):
    lower_weight, upper_weight = filter_weights(thickness, level_cuts)
    zero_row = jnp.zeros_like(values[:, :1, :])
    below = jnp.concatenate([zero_row, values[:, :-1, :]], axis=1)
    above = jnp.concatenate([values[:, 1:, :], zero_row], axis=1)
    numer = (
        2.0 * thickness[None, :, None] * values
        + lower_weight[None, :, None] * below
        + upper_weight[None, :, None] * above
    )
    denom = 2.0 * thickness + lower_weight + upper_weight
    return numer / denom[None, :, None]


def quadratic_features(smooth):
    count = smooth.shape[2]
    later = jnp.concatenate([smooth[2], smooth[3]], axis=0)
    earlier = jnp.concatenate([smooth[0], smooth[1]], axis=0)
    product = (later[:, None, :] * smooth[0][None, :, :]).reshape(-1, count)
    return jnp.concatenate([later, earlier, product], axis=0).astype(jnp.bfloat16)


def general_plan(slab_fields, sample_index, thickness, level_cuts):
    samp_count = sample_index.shape[1]
    lev_count = lax.axis_size("lev")
    hor_count = lax.axis_size("hor")
    all_lists = lax.all_gather(sample_index, "lev", axis=1, tiled=True)[0]
    group_cols = slab_fields.shape[2] // lev_count
    offsets = jnp.arange(all_lists.shape[0]) // samp_count * group_cols + all_lists
    chosen = jnp.take(slab_fields, offsets, axis=2)
    picked_cols = lax.all_to_all(chosen, "lev", split_axis=2, concat_axis=1, tiled=True)
    smooth = vertical_filter(picked_cols, thickness, level_cuts)
    feat_count = 4 * smooth.shape[1] + 2 * smooth.shape[1] * smooth.shape[1]
    col_count = feat_count // lev_count
    col_start = lax.axis_index("lev") * col_count
    features_bf = quadratic_features(smooth)
    block_features_bf = lax.all_gather(features_bf, "lev", axis=1, tiled=True)
    chosen_rows = lax.dynamic_slice_in_dim(block_features_bf, col_start, col_count, 0)
    column_block = lax.dot_general(
        block_features_bf, chosen_rows, (((1,), (1,)), ((), ())), preferred_element_type=jnp.float32
    )
    gram_block = lax.psum_scatter(column_block, "hor", scatter_dimension=0, tiled=True)
    count_all = samp_count * lev_count * hor_count
    return gram_block / count_all


def gram_kernel(
    slab_hbm, idx_hbm, thick_hbm, cuts_hbm, out_ref,
    slab_ref, idx_ref, thick_ref, cuts_ref, coef_ref, buf, other_idx,
    later_ref, rows_ref, lhs_ref, cols_ref, recv_sem, send_sem, idx_sem, local_sem,
):
    group_cols = slab_ref.shape[2] // 2
    x = lax.axis_index("lev")
    h = lax.axis_index("hor")
    z, y, c = h // 4, h // 2 % 2, h % 2

    def along_z(k):
        return (z // 2 + k // 2) % 2 * 2 + (z + k) % 2

    def place(zz, yy, cc):
        return zz * 4 + yy * 2 + cc

    def piece(xx, hh, g):
        return (xx * 16 + hh) * 2 + g

    x_mate = (1 - x, h)
    y_mate = (x, place(z, 1 - y, c))
    core_mate = (x, place(z, y, 1 - c))
    z_mates = [(x, place(along_z(k), y, c)) for k in (1, 2, 3)]

    def send(p, target):
        pltpu.make_async_remote_copy(
            src_ref=buf.at[p], dst_ref=buf.at[p], send_sem=send_sem, recv_sem=recv_sem.at[p],
            device_id=target, device_id_type=MESH,
        ).start()

    def arrive(p):
        pltpu.make_async_copy(buf.at[p], buf.at[p], recv_sem.at[p]).wait()

    def load_group(g, sem):
        cols = pl.ds(pl.multiple_of(g * group_cols, group_cols), group_cols)
        return pltpu.make_async_copy(slab_hbm.at[:, :, cols], slab_ref.at[:, :, cols], sem)

    idx_load = pltpu.make_async_copy(idx_hbm, idx_ref, local_sem.at[0])
    thick_load = pltpu.make_async_copy(thick_hbm, thick_ref, local_sem.at[1])
    cuts_load = pltpu.make_async_copy(cuts_hbm, cuts_ref, local_sem.at[2])
    own_load = load_group(x, local_sem.at[3])
    other_load = load_group(1 - x, local_sem.at[4])
    for load in (idx_load, own_load, thick_load, cuts_load, other_load):
        load.start()

    barrier = pltpu.get_barrier_semaphore()
    for mate in [x_mate, y_mate, core_mate] + z_mates:
        pl.semaphore_signal(barrier, inc=1, device_id=mate, device_id_type=MESH)
    out_ref[...] = jnp.zeros_like(out_ref)
    lhs_ref[1] = jnp.zeros((136, 256), jnp.float32)
    cols_ref[1] = jnp.zeros((1088, 256), jnp.bfloat16)
    pl.semaphore_wait(barrier, 6)

    idx_copy = pltpu.make_async_remote_copy(
        src_ref=idx_hbm, dst_ref=other_idx, send_sem=idx_sem.at[0], recv_sem=idx_sem.at[1],
        device_id=x_mate, device_id_type=MESH,
    )
    idx_copy.start()

    def pick(g, idx_row):
        step = 512
        total = jnp.zeros((192, 128), jnp.float32)
        for t in range(group_cols // step):
            start = pl.multiple_of(g * group_cols + t * step, step)
            v = slab_ref[:, :, pl.ds(start, step)].reshape(64, step)
            hi = v.astype(jnp.bfloat16)
            rest = v - hi.astype(jnp.float32)
            mid = rest.astype(jnp.bfloat16)
            low = (rest - mid.astype(jnp.float32)).astype(jnp.bfloat16)
            parts = jnp.concatenate([hi, mid, low], axis=0)
            lane = lax.broadcasted_iota(jnp.int32, (step, 128), 0) + t * step
            hot = jnp.where(lane == idx_row, 1.0, 0.0).astype(jnp.bfloat16)
            total += jnp.dot(parts, hot, preferred_element_type=jnp.float32)
        p = piece(x, h, g)
        buf[p] = total[0:64] + total[64:128] + total[128:192]
        for mate in z_mates + [x_mate, y_mate, core_mate]:
            send(p, mate)

    idx_load.wait()
    own_load.wait()
    pick(x, idx_ref[...])
    other_load.wait()
    idx_copy.wait_recv()
    pick(1 - x, other_idx[...])

    thick_load.wait()
    cuts_load.wait()

    def column(row, shift):
        shape = (32, row.shape[1])
        level = lax.broadcasted_iota(jnp.int32, shape, 0) + shift
        hit = level == lax.broadcasted_iota(jnp.int32, shape, 1)
        return jnp.sum(jnp.where(hit, row, 0.0), axis=1, keepdims=True)

    thick = thick_ref[...]
    link = 1.0 - cuts_ref[...].astype(jnp.float32)
    weights = [
        2.0 * column(thick, 0),
        column(thick, -1) * column(link, -1),
        column(thick, 1) * column(link, 0),
    ]
    denom = weights[0] + weights[1] + weights[2]
    for i in range(3):
        coef_ref[i] = jnp.broadcast_to(weights[i] / denom, (32, 128))

    def forward_z(i, carry):
        g = (x + i) % 2
        p = piece(x, place(along_z(1 + i // 2), y, c), g)
        arrive(p)
        for mate in [x_mate, y_mate, core_mate]:
            send(p, mate)
        return carry

    lax.fori_loop(0, 6, forward_z, 0)

    past_first = (h + 15) // 16
    first_row = (136 * h - 128) * past_first
    first_m = first_row // 32
    row_start = pl.multiple_of(past_first * (128 + first_row - 32 * first_m), 8)

    def features(hh, slot):
        for g in range(2):
            lanes = slice(g * 128, g * 128 + 128)
            below_p, above_p = piece(0, hh, g), piece(1, hh, g)
            smooth = []
            for f in range(4):
                levels = slice(16 * f, 16 * f + 16)
                v = jnp.concatenate([buf[below_p, levels, :], buf[above_p, levels, :]], axis=0)
                smooth.append(
                    coef_ref[0] * v
                    + coef_ref[1] * pltpu.roll(v, 1, 0)
                    + coef_ref[2] * pltpu.roll(v, 31, 0)
                )
            base = smooth[0]
            later_ref[slot, g, 0:32, :] = smooth[2]
            later_ref[slot, g, 32:64, :] = smooth[3]
            direct = [smooth[2], smooth[3], smooth[0], smooth[1]]
            for b in range(4):
                rows_ref[slot, 32 * b:32 * b + 32, lanes] = direct[b]
            for i in range(5):
                m_row = later_ref[slot, g, pl.ds(first_m + i, 1), :]
                rows_ref[slot, 128 + 32 * i:160 + 32 * i, lanes] = m_row * base
            for b in range(34):
                if b < 4:
                    m_row = later_ref[slot, g, 30 + b:31 + b, :]
                    block = jnp.where(x == 0, direct[b], m_row * base)
                else:
                    m_row = later_ref[slot, g, pl.ds(b - 4 + 34 * x, 1), :]
                    block = m_row * base
                cols_ref[slot, 32 * b:32 * b + 32, lanes] = block.astype(jnp.bfloat16)
        lhs_ref[slot] = rows_ref[slot, pl.ds(row_start, 136), :]

    def add_product(slot):
        out_ref[...] += lax.dot_general(
            lhs_ref[slot].astype(jnp.bfloat16), cols_ref[slot],
            (((1,), (1,)), ((), ())), preferred_element_type=jnp.float32,
        )

    def spread_near(k):
        zz = along_z(k)
        near, across = place(zz, y, c), place(zz, 1 - y, c)
        p = piece(1 - x, near, 1)
        arrive(p)
        send(p, y_mate)
        send(p, core_mate)
        p = piece(x, across, 0)
        arrive(p)
        send(p, x_mate)
        send(p, core_mate)
        for p in (piece(1 - x, near, 0), piece(x, across, 1)):
            arrive(p)
            send(p, core_mate)

    def spread_far(k):
        for g in range(2):
            p = piece(1 - x, place(along_z(k), 1 - y, c), g)
            arrive(p)
            send(p, core_mate)

    def step(u, carry):
        for half in range(2):
            j = 2 * u + half

            @pl.when(u < 2)
            def _():
                spread_near(j)

            @pl.when((u - 1) // 2 == 1)
            def _():
                spread_far(j - 6)

            far = j // 8
            mate = (1 - far) * (j // 4 % 2) + far * (j // 2 % 2)
            k = (1 - far) * (j % 4) + far * (j % 8 // 4 * 2 + j % 2)
            hh = place(along_z(k), (y + far) % 2, (c + mate) % 2)

            @pl.when(mate == 1)
            def _():
                for xx in range(2):
                    for g in range(2):
                        arrive(piece(xx, hh, g))

            features(hh, half)
            add_product(1 - half)
        return carry

    lax.fori_loop(0, 8, step, 0)
    add_product(1)
    out_ref[...] = out_ref[...] * (1.0 / 4096)
    sent = buf.at[pl.ds(0, 62)]
    pltpu.make_async_copy(sent, sent, send_sem).wait()
    idx_copy.wait_send()


def on_slice(slab_fields, sample_index, thickness, level_cuts):
    return pl.pallas_call(
        gram_kernel,
        out_shape=jax.ShapeDtypeStruct((136, 1088), jnp.float32),
        in_specs=[pl.BlockSpec(memory_space=pltpu.HBM)] * 4,
        out_specs=pl.BlockSpec(memory_space=pltpu.VMEM),
        scratch_shapes=[
            pltpu.VMEM(slab_fields.shape, jnp.float32),
            pltpu.VMEM((1, 128), jnp.int32),
            pltpu.VMEM((1, 32), jnp.float32),
            pltpu.VMEM((1, 31), jnp.int32),
            pltpu.VMEM((3, 32, 128), jnp.float32),
            pltpu.VMEM((64, 64, 128), jnp.float32),
            pltpu.VMEM((1, 128), jnp.int32),
            pltpu.VMEM((2, 2, 64, 128), jnp.float32),
            pltpu.VMEM((2, 288, 256), jnp.float32),
            pltpu.VMEM((2, 136, 256), jnp.float32),
            pltpu.VMEM((2, 1088, 256), jnp.bfloat16),
            pltpu.SemaphoreType.DMA((64,)),
            pltpu.SemaphoreType.DMA,
            pltpu.SemaphoreType.DMA((2,)),
            pltpu.SemaphoreType.DMA((5,)),
        ],
        compiler_params=pltpu.CompilerParams(
            collective_id=0, has_side_effects=True, vmem_limit_bytes=60 * 1024 * 1024
        ),
    )(slab_fields, sample_index, thickness[None, :], level_cuts[None, :])


def solution(mesh):
    in_specs = (P(None, "lev", "hor"), P("hor", "lev"), P(), P())
    out_specs = P("hor", "lev")
    small = mesh.shape["lev"] == 2 and mesh.shape["hor"] == 16
    return jax.shard_map(
        on_slice if small else general_plan,
        mesh=mesh, in_specs=in_specs, out_specs=out_specs, check_vma=False,
    )
```

```python
import jax
import jax.numpy as jnp
from jax import lax
from jax.experimental import pallas as pl
from jax.experimental.pallas import tpu as pltpu
from jax.sharding import PartitionSpec as P

MESH = pl.DeviceIdType.MESH


def filter_weights(thickness, level_cuts):
    link = 1.0 - level_cuts.astype(jnp.float32)
    zero_one = jnp.zeros((1,), jnp.float32)
    lower_link = jnp.concatenate([zero_one, link])
    upper_link = jnp.concatenate([link, zero_one])
    lower_weight = jnp.concatenate([zero_one, thickness[:-1]]) * lower_link
    upper_weight = jnp.concatenate([thickness[1:], zero_one]) * upper_link
    return lower_weight, upper_weight


def vertical_filter(values, thickness, level_cuts):
    lower_weight, upper_weight = filter_weights(thickness, level_cuts)
    zero_row = jnp.zeros_like(values[:, :1, :])
    below = jnp.concatenate([zero_row, values[:, :-1, :]], axis=1)
    above = jnp.concatenate([values[:, 1:, :], zero_row], axis=1)
    numer = (
        2.0 * thickness[None, :, None] * values
        + lower_weight[None, :, None] * below
        + upper_weight[None, :, None] * above
    )
    denom = 2.0 * thickness + lower_weight + upper_weight
    return numer / denom[None, :, None]


def quadratic_features(smooth):
    count = smooth.shape[2]
    later = jnp.concatenate([smooth[2], smooth[3]], axis=0)
    earlier = jnp.concatenate([smooth[0], smooth[1]], axis=0)
    product = (later[:, None, :] * smooth[0][None, :, :]).reshape(-1, count)
    return jnp.concatenate([later, earlier, product], axis=0).astype(jnp.bfloat16)


def general_plan(slab_fields, sample_index, thickness, level_cuts):
    samp_count = sample_index.shape[1]
    lev_count = lax.axis_size("lev")
    hor_count = lax.axis_size("hor")
    all_lists = lax.all_gather(sample_index, "lev", axis=1, tiled=True)[0]
    group_cols = slab_fields.shape[2] // lev_count
    offsets = jnp.arange(all_lists.shape[0]) // samp_count * group_cols + all_lists
    chosen = jnp.take(slab_fields, offsets, axis=2)
    picked_cols = lax.all_to_all(chosen, "lev", split_axis=2, concat_axis=1, tiled=True)
    smooth = vertical_filter(picked_cols, thickness, level_cuts)
    feat_count = 4 * smooth.shape[1] + 2 * smooth.shape[1] * smooth.shape[1]
    col_count = feat_count // lev_count
    col_start = lax.axis_index("lev") * col_count
    features_bf = quadratic_features(smooth)
    block_features_bf = lax.all_gather(features_bf, "lev", axis=1, tiled=True)
    chosen_rows = lax.dynamic_slice_in_dim(block_features_bf, col_start, col_count, 0)
    column_block = lax.dot_general(
        block_features_bf, chosen_rows, (((1,), (1,)), ((), ())), preferred_element_type=jnp.float32
    )
    gram_block = lax.psum_scatter(column_block, "hor", scatter_dimension=0, tiled=True)
    count_all = samp_count * lev_count * hor_count
    return gram_block / count_all


def gram_kernel(
    slab_hbm, idx_hbm, thick_hbm, cuts_hbm, out_ref,
    slab_ref, idx_ref, thick_ref, cuts_ref, coef_ref, buf, other_idx,
    later_ref, rows_ref, lhs_ref, cols_ref, acc_ref, recv_sem, send_sem, idx_sem, local_sem,
):
    group_cols = slab_ref.shape[2] // 2
    x = lax.axis_index("lev")
    h = lax.axis_index("hor")
    z, y, c = h // 4, h // 2 % 2, h % 2

    def along_z(k):
        return (z // 2 + k // 2) % 2 * 2 + (z + k) % 2

    def place(zz, yy, cc):
        return zz * 4 + yy * 2 + cc

    def piece(xx, hh, g):
        return (xx * 16 + hh) * 2 + g

    x_mate = (1 - x, h)
    y_mate = (x, place(z, 1 - y, c))
    core_mate = (x, place(z, y, 1 - c))
    z_mates = [(x, place(along_z(k), y, c)) for k in (1, 2, 3)]

    def send(p, target):
        pltpu.make_async_remote_copy(
            src_ref=buf.at[p], dst_ref=buf.at[p], send_sem=send_sem, recv_sem=recv_sem.at[p],
            device_id=target, device_id_type=MESH,
        ).start()

    def arrive(p):
        pltpu.make_async_copy(buf.at[p], buf.at[p], recv_sem.at[p]).wait()

    def load_group(g, sem):
        cols = pl.ds(pl.multiple_of(g * group_cols, group_cols), group_cols)
        return pltpu.make_async_copy(slab_hbm.at[:, :, cols], slab_ref.at[:, :, cols], sem)

    idx_load = pltpu.make_async_copy(idx_hbm, idx_ref, local_sem.at[0])
    thick_load = pltpu.make_async_copy(thick_hbm, thick_ref, local_sem.at[1])
    cuts_load = pltpu.make_async_copy(cuts_hbm, cuts_ref, local_sem.at[2])
    own_load = load_group(x, local_sem.at[3])
    other_load = load_group(1 - x, local_sem.at[4])
    for load in (idx_load, own_load, thick_load, cuts_load, other_load):
        load.start()

    barrier = pltpu.get_barrier_semaphore()
    for mate in [x_mate, y_mate, core_mate] + z_mates:
        pl.semaphore_signal(barrier, inc=1, device_id=mate, device_id_type=MESH)
    acc_ref[...] = jnp.zeros_like(acc_ref)
    lhs_ref[1] = jnp.zeros((136, 256), jnp.float32)
    cols_ref[1] = jnp.zeros((1088, 256), jnp.bfloat16)
    pl.semaphore_wait(barrier, 6)

    idx_copy = pltpu.make_async_remote_copy(
        src_ref=idx_hbm, dst_ref=other_idx, send_sem=idx_sem.at[0], recv_sem=idx_sem.at[1],
        device_id=x_mate, device_id_type=MESH,
    )
    idx_copy.start()

    def pick(g, idx_row):
        step = 512
        total = jnp.zeros((192, 128), jnp.float32)
        for t in range(group_cols // step):
            start = pl.multiple_of(g * group_cols + t * step, step)
            v = slab_ref[:, :, pl.ds(start, step)].reshape(64, step)
            hi = v.astype(jnp.bfloat16)
            rest = v - hi.astype(jnp.float32)
            mid = rest.astype(jnp.bfloat16)
            low = (rest - mid.astype(jnp.float32)).astype(jnp.bfloat16)
            parts = jnp.concatenate([hi, mid, low], axis=0)
            lane = lax.broadcasted_iota(jnp.int32, (step, 128), 0) + t * step
            hot = jnp.where(lane == idx_row, 1.0, 0.0).astype(jnp.bfloat16)
            total += jnp.dot(parts, hot, preferred_element_type=jnp.float32)
        p = piece(x, h, g)
        buf[p] = total[0:64] + total[64:128] + total[128:192]
        for mate in z_mates + [x_mate, y_mate, core_mate]:
            send(p, mate)

    idx_load.wait()
    own_load.wait()
    pick(x, idx_ref[...])
    other_load.wait()
    idx_copy.wait_recv()
    pick(1 - x, other_idx[...])

    thick_load.wait()
    cuts_load.wait()

    def column(row, shift):
        shape = (32, row.shape[1])
        level = lax.broadcasted_iota(jnp.int32, shape, 0) + shift
        hit = level == lax.broadcasted_iota(jnp.int32, shape, 1)
        return jnp.sum(jnp.where(hit, row, 0.0), axis=1, keepdims=True)

    thick = thick_ref[...]
    link = 1.0 - cuts_ref[...].astype(jnp.float32)
    weights = [
        2.0 * column(thick, 0),
        column(thick, -1) * column(link, -1),
        column(thick, 1) * column(link, 0),
    ]
    denom = weights[0] + weights[1] + weights[2]
    for i in range(3):
        coef_ref[i] = jnp.broadcast_to(weights[i] / denom, (32, 128))

    def forward_z(i, carry):
        g = (x + i) % 2
        p = piece(x, place(along_z(1 + i // 2), y, c), g)
        arrive(p)
        for mate in [x_mate, y_mate, core_mate]:
            send(p, mate)
        return carry

    lax.fori_loop(0, 6, forward_z, 0)

    past_first = (h + 15) // 16
    first_row = (136 * h - 128) * past_first
    first_m = first_row // 32
    row_start = pl.multiple_of(past_first * (128 + first_row - 32 * first_m), 8)

    def features(hh, slot):
        for g in range(2):
            lanes = slice(g * 128, g * 128 + 128)
            below_p, above_p = piece(0, hh, g), piece(1, hh, g)
            smooth = []
            for f in range(4):
                levels = slice(16 * f, 16 * f + 16)
                v = jnp.concatenate([buf[below_p, levels, :], buf[above_p, levels, :]], axis=0)
                smooth.append(
                    coef_ref[0] * v
                    + coef_ref[1] * pltpu.roll(v, 1, 0)
                    + coef_ref[2] * pltpu.roll(v, 31, 0)
                )
            base = smooth[0]
            later_ref[slot, g, 0:32, :] = smooth[2]
            later_ref[slot, g, 32:64, :] = smooth[3]
            direct = [smooth[2], smooth[3], smooth[0], smooth[1]]
            for b in range(4):
                rows_ref[slot, 32 * b:32 * b + 32, lanes] = direct[b]
            for i in range(5):
                m_row = later_ref[slot, g, pl.ds(first_m + i, 1), :]
                rows_ref[slot, 128 + 32 * i:160 + 32 * i, lanes] = m_row * base
            for b in range(34):
                if b < 4:
                    m_row = later_ref[slot, g, 30 + b:31 + b, :]
                    block = jnp.where(x == 0, direct[b], m_row * base)
                else:
                    m_row = later_ref[slot, g, pl.ds(b - 4 + 34 * x, 1), :]
                    block = m_row * base
                cols_ref[slot, 32 * b:32 * b + 32, lanes] = block.astype(jnp.bfloat16)
        lhs_ref[slot] = rows_ref[slot, pl.ds(row_start, 136), :]

    def add_product(slot):
        acc_ref[...] += lax.dot_general(
            cols_ref[slot], lhs_ref[slot].astype(jnp.bfloat16),
            (((1,), (1,)), ((), ())), preferred_element_type=jnp.float32,
        )

    def spread_near(k):
        zz = along_z(k)
        near, across = place(zz, y, c), place(zz, 1 - y, c)
        p = piece(1 - x, near, 1)
        arrive(p)
        send(p, y_mate)
        send(p, core_mate)
        p = piece(x, across, 0)
        arrive(p)
        send(p, x_mate)
        send(p, core_mate)
        for p in (piece(1 - x, near, 0), piece(x, across, 1)):
            arrive(p)
            send(p, core_mate)

    def spread_far(k):
        for g in range(2):
            p = piece(1 - x, place(along_z(k), 1 - y, c), g)
            arrive(p)
            send(p, core_mate)

    def step(u, carry):
        for half in range(2):
            j = 2 * u + half

            @pl.when(u < 2)
            def _():
                spread_near(j)

            @pl.when((u - 1) // 2 == 1)
            def _():
                spread_far(j - 6)

            far = j // 8
            mate = (1 - far) * (j // 4 % 2) + far * (j // 2 % 2)
            k = (1 - far) * (j % 4) + far * (j % 8 // 4 * 2 + j % 2)
            hh = place(along_z(k), (y + far) % 2, (c + mate) % 2)

            @pl.when(mate == 1)
            def _():
                for xx in range(2):
                    for g in range(2):
                        arrive(piece(xx, hh, g))

            features(hh, half)
            add_product(1 - half)
        return carry

    lax.fori_loop(0, 8, step, 0)
    add_product(1)
    out_ref[...] = acc_ref[...].T * (1.0 / 4096)
    sent = buf.at[pl.ds(0, 62)]
    pltpu.make_async_copy(sent, sent, send_sem).wait()
    idx_copy.wait_send()


def on_slice(slab_fields, sample_index, thickness, level_cuts):
    return pl.pallas_call(
        gram_kernel,
        out_shape=jax.ShapeDtypeStruct((136, 1088), jnp.float32),
        in_specs=[pl.BlockSpec(memory_space=pltpu.HBM)] * 4,
        out_specs=pl.BlockSpec(memory_space=pltpu.VMEM),
        scratch_shapes=[
            pltpu.VMEM(slab_fields.shape, jnp.float32),
            pltpu.VMEM((1, 128), jnp.int32),
            pltpu.VMEM((1, 32), jnp.float32),
            pltpu.VMEM((1, 31), jnp.int32),
            pltpu.VMEM((3, 32, 128), jnp.float32),
            pltpu.VMEM((64, 64, 128), jnp.float32),
            pltpu.VMEM((1, 128), jnp.int32),
            pltpu.VMEM((2, 2, 64, 128), jnp.float32),
            pltpu.VMEM((2, 288, 256), jnp.float32),
            pltpu.VMEM((2, 136, 256), jnp.float32),
            pltpu.VMEM((2, 1088, 256), jnp.bfloat16),
            pltpu.VMEM((1088, 136), jnp.float32),
            pltpu.SemaphoreType.DMA((64,)),
            pltpu.SemaphoreType.DMA,
            pltpu.SemaphoreType.DMA((2,)),
            pltpu.SemaphoreType.DMA((5,)),
        ],
        compiler_params=pltpu.CompilerParams(
            collective_id=0, has_side_effects=True, vmem_limit_bytes=53 * 1024 * 1024
        ),
    )(slab_fields, sample_index, thickness[None, :], level_cuts[None, :])


def solution(mesh):
    in_specs = (P(None, "lev", "hor"), P("hor", "lev"), P(), P())
    out_specs = P("hor", "lev")
    small = mesh.shape["lev"] == 2 and mesh.shape["hor"] == 16
    return jax.shard_map(
        on_slice if small else general_plan,
        mesh=mesh, in_specs=in_specs, out_specs=out_specs, check_vma=False,
    )
```

```python
import jax
import jax.numpy as jnp
from jax import lax
from jax.experimental import pallas as pl
from jax.experimental.pallas import tpu as pltpu
from jax.sharding import PartitionSpec as P

MESH = pl.DeviceIdType.MESH


def filter_weights(thickness, level_cuts):
    link = 1.0 - level_cuts.astype(jnp.float32)
    zero_one = jnp.zeros((1,), jnp.float32)
    lower_link = jnp.concatenate([zero_one, link])
    upper_link = jnp.concatenate([link, zero_one])
    lower_weight = jnp.concatenate([zero_one, thickness[:-1]]) * lower_link
    upper_weight = jnp.concatenate([thickness[1:], zero_one]) * upper_link
    return lower_weight, upper_weight


def vertical_filter(values, thickness, level_cuts):
    lower_weight, upper_weight = filter_weights(thickness, level_cuts)
    zero_row = jnp.zeros_like(values[:, :1, :])
    below = jnp.concatenate([zero_row, values[:, :-1, :]], axis=1)
    above = jnp.concatenate([values[:, 1:, :], zero_row], axis=1)
    numer = (
        2.0 * thickness[None, :, None] * values
        + lower_weight[None, :, None] * below
        + upper_weight[None, :, None] * above
    )
    denom = 2.0 * thickness + lower_weight + upper_weight
    return numer / denom[None, :, None]


def quadratic_features(smooth):
    count = smooth.shape[2]
    later = jnp.concatenate([smooth[2], smooth[3]], axis=0)
    earlier = jnp.concatenate([smooth[0], smooth[1]], axis=0)
    product = (later[:, None, :] * smooth[0][None, :, :]).reshape(-1, count)
    return jnp.concatenate([later, earlier, product], axis=0).astype(jnp.bfloat16)


def general_plan(slab_fields, sample_index, thickness, level_cuts):
    samp_count = sample_index.shape[1]
    lev_count = lax.axis_size("lev")
    hor_count = lax.axis_size("hor")
    all_lists = lax.all_gather(sample_index, "lev", axis=1, tiled=True)[0]
    group_cols = slab_fields.shape[2] // lev_count
    offsets = jnp.arange(all_lists.shape[0]) // samp_count * group_cols + all_lists
    chosen = jnp.take(slab_fields, offsets, axis=2)
    picked_cols = lax.all_to_all(chosen, "lev", split_axis=2, concat_axis=1, tiled=True)
    smooth = vertical_filter(picked_cols, thickness, level_cuts)
    feat_count = 4 * smooth.shape[1] + 2 * smooth.shape[1] * smooth.shape[1]
    col_count = feat_count // lev_count
    col_start = lax.axis_index("lev") * col_count
    features_bf = quadratic_features(smooth)
    block_features_bf = lax.all_gather(features_bf, "lev", axis=1, tiled=True)
    chosen_rows = lax.dynamic_slice_in_dim(block_features_bf, col_start, col_count, 0)
    column_block = lax.dot_general(
        block_features_bf, chosen_rows, (((1,), (1,)), ((), ())), preferred_element_type=jnp.float32
    )
    gram_block = lax.psum_scatter(column_block, "hor", scatter_dimension=0, tiled=True)
    count_all = samp_count * lev_count * hor_count
    return gram_block / count_all


def gram_kernel(
    slab_hbm, idx_hbm, thick_hbm, cuts_hbm, out_ref,
    slab_ref, idx_ref, thick_ref, cuts_ref, coef_ref, buf, other_idx,
    rows_ref, cols_ref, recv_sem, send_sem, idx_sem, local_sem,
):
    group_cols = slab_ref.shape[2] // 2
    x = lax.axis_index("lev")
    h = lax.axis_index("hor")
    z, y, c = h // 4, h // 2 % 2, h % 2

    def along_z(k):
        return (z // 2 + k // 2) % 2 * 2 + (z + k) % 2

    def place(zz, yy, cc):
        return zz * 4 + yy * 2 + cc

    def piece(xx, hh, g):
        return (xx * 16 + hh) * 2 + g

    x_mate = (1 - x, h)
    y_mate = (x, place(z, 1 - y, c))
    core_mate = (x, place(z, y, 1 - c))
    z_mates = [(x, place(along_z(k), y, c)) for k in (1, 2, 3)]

    def send(p, target):
        pltpu.make_async_remote_copy(
            src_ref=buf.at[p], dst_ref=buf.at[p], send_sem=send_sem, recv_sem=recv_sem.at[p],
            device_id=target, device_id_type=MESH,
        ).start()

    def arrive(p):
        pltpu.make_async_copy(buf.at[p], buf.at[p], recv_sem.at[p]).wait()

    def load_group(g, sem):
        cols = pl.ds(pl.multiple_of(g * group_cols, group_cols), group_cols)
        return pltpu.make_async_copy(slab_hbm.at[:, :, cols], slab_ref.at[:, :, cols], sem)

    idx_load = pltpu.make_async_copy(idx_hbm, idx_ref, local_sem.at[0])
    thick_load = pltpu.make_async_copy(thick_hbm, thick_ref, local_sem.at[1])
    cuts_load = pltpu.make_async_copy(cuts_hbm, cuts_ref, local_sem.at[2])
    own_load = load_group(x, local_sem.at[3])
    other_load = load_group(1 - x, local_sem.at[4])
    for load in (idx_load, own_load, thick_load, cuts_load, other_load):
        load.start()

    barrier = pltpu.get_barrier_semaphore()
    for mate in [x_mate, y_mate, core_mate] + z_mates:
        pl.semaphore_signal(barrier, inc=1, device_id=mate, device_id_type=MESH)
    out_ref[...] = jnp.zeros_like(out_ref)
    rows_ref[1] = jnp.zeros((4, 288, 128), jnp.float32)
    cols_ref[1] = jnp.zeros((1088, 512), jnp.bfloat16)
    pl.semaphore_wait(barrier, 6)

    idx_copy = pltpu.make_async_remote_copy(
        src_ref=idx_hbm, dst_ref=other_idx, send_sem=idx_sem.at[0], recv_sem=idx_sem.at[1],
        device_id=x_mate, device_id_type=MESH,
    )
    idx_copy.start()

    def pick(g, idx_row):
        step = 512
        total = jnp.zeros((192, 128), jnp.float32)
        for t in range(group_cols // step):
            start = pl.multiple_of(g * group_cols + t * step, step)
            v = slab_ref[:, :, pl.ds(start, step)].reshape(64, step)
            hi = v.astype(jnp.bfloat16)
            rest = v - hi.astype(jnp.float32)
            mid = rest.astype(jnp.bfloat16)
            low = (rest - mid.astype(jnp.float32)).astype(jnp.bfloat16)
            parts = jnp.concatenate([hi, mid, low], axis=0)
            lane = lax.broadcasted_iota(jnp.int32, (step, 128), 0) + t * step
            hot = jnp.where(lane == idx_row, 1.0, 0.0).astype(jnp.bfloat16)
            total += jnp.dot(parts, hot, preferred_element_type=jnp.float32)
        p = piece(x, h, g)
        buf[p] = total[0:64] + total[64:128] + total[128:192]
        for mate in [x_mate, y_mate] + z_mates + [core_mate]:
            send(p, mate)

    idx_load.wait()
    own_load.wait()
    pick(x, idx_ref[...])
    other_load.wait()
    idx_copy.wait_recv()
    pick(1 - x, other_idx[...])

    thick_load.wait()
    cuts_load.wait()

    def column(row, shift):
        shape = (32, row.shape[1])
        level = lax.broadcasted_iota(jnp.int32, shape, 0) + shift
        hit = level == lax.broadcasted_iota(jnp.int32, shape, 1)
        return jnp.sum(jnp.where(hit, row, 0.0), axis=1, keepdims=True)

    thick = thick_ref[...]
    link = 1.0 - cuts_ref[...].astype(jnp.float32)
    weights = [
        2.0 * column(thick, 0),
        column(thick, -1) * column(link, -1),
        column(thick, 1) * column(link, 0),
    ]
    denom = weights[0] + weights[1] + weights[2]
    for i in range(3):
        coef_ref[i] = jnp.broadcast_to(weights[i] / denom, (32, 128))

    def forward_z(i, carry):
        g = (x + i) % 2
        p = piece(x, place(along_z(1 + i // 2), y, c), g)
        arrive(p)
        for mate in [x_mate, y_mate, core_mate]:
            send(p, mate)
        return carry

    lax.fori_loop(0, 6, forward_z, 0)

    past_first = (h + 15) // 16
    first_row = (136 * h - 128) * past_first
    first_m = first_row // 32
    row_start = pl.multiple_of(past_first * (128 + first_row - 32 * first_m), 8)

    def features(hh, slot, half):
        for g in range(2):
            lanes = slice(half * 256 + g * 128, half * 256 + g * 128 + 128)
            q = half * 2 + g
            below_p, above_p = piece(0, hh, g), piece(1, hh, g)
            smooth = []
            for f in range(4):
                levels = slice(16 * f, 16 * f + 16)
                v = jnp.concatenate([buf[below_p, levels, :], buf[above_p, levels, :]], axis=0)
                smooth.append(
                    coef_ref[0] * v
                    + coef_ref[1] * pltpu.roll(v, 1, 0)
                    + coef_ref[2] * pltpu.roll(v, 31, 0)
                )
            base = smooth[0]
            direct = [smooth[2], smooth[3], smooth[0], smooth[1]]
            for b in range(4):
                rows_ref[slot, q, 32 * b:32 * b + 32, :] = direct[b]
            for i in range(5):
                m_row = rows_ref[slot, q, pl.ds(first_m + i, 1), :]
                rows_ref[slot, q, 128 + 32 * i:160 + 32 * i, :] = m_row * base
            chosen = jnp.where(x == 0, smooth[2], pltpu.roll(smooth[3], 30, 0))
            for b in range(34):
                if b < 2:
                    block = jnp.where(x == 0, direct[b], smooth[2][30 + b:31 + b] * base)
                elif b < 4:
                    block = jnp.where(x == 0, direct[b], smooth[3][b - 2:b - 1] * base)
                else:
                    block = chosen[b - 4:b - 3] * base
                cols_ref[slot, 32 * b:32 * b + 32, lanes] = block.astype(jnp.bfloat16)

    def add_product(slot):
        own = [rows_ref[slot, q, pl.ds(row_start, 136), :] for q in range(4)]
        out_ref[...] += lax.dot_general(
            jnp.concatenate(own, axis=1).astype(jnp.bfloat16), cols_ref[slot],
            (((1,), (1,)), ((), ())), preferred_element_type=jnp.float32,
        )

    def spread_near(k):
        zz = along_z(k)
        near, across = place(zz, y, c), place(zz, 1 - y, c)
        p = piece(1 - x, near, 1)
        arrive(p)
        send(p, y_mate)
        send(p, core_mate)
        p = piece(x, across, 0)
        arrive(p)
        send(p, x_mate)
        send(p, core_mate)
        for p in (piece(1 - x, near, 0), piece(x, across, 1)):
            arrive(p)
            send(p, core_mate)

    def spread_far(k):
        for g in range(2):
            p = piece(1 - x, place(along_z(k), 1 - y, c), g)
            arrive(p)
            send(p, core_mate)

    def step(u, carry):
        for part in range(4):
            j = 4 * u + part

            @pl.when(u == 0)
            def _():
                spread_near(j)

            @pl.when((j + 2) // 4 == 2)
            def _():
                spread_far(j - 6)

            far = j // 8
            mate = (1 - far) * (j // 4 % 2) + far * (j // 2 % 2)
            k = (1 - far) * (j % 4) + far * (j % 8 // 4 * 2 + j % 2)
            hh = place(along_z(k), (y + far) % 2, (c + mate) % 2)

            @pl.when(mate == 1)
            def _():
                for xx in range(2):
                    for g in range(2):
                        arrive(piece(xx, hh, g))

            features(hh, part // 2, part % 2)
            if part % 2 == 1:
                add_product(1 - part // 2)
        return carry

    lax.fori_loop(0, 4, step, 0)
    add_product(1)
    out_ref[...] = out_ref[...] * (1.0 / 4096)
    sent = buf.at[pl.ds(0, 62)]
    pltpu.make_async_copy(sent, sent, send_sem).wait()
    idx_copy.wait_send()


def on_slice(slab_fields, sample_index, thickness, level_cuts):
    return pl.pallas_call(
        gram_kernel,
        out_shape=jax.ShapeDtypeStruct((136, 1088), jnp.float32),
        in_specs=[pl.BlockSpec(memory_space=pltpu.HBM)] * 4,
        out_specs=pl.BlockSpec(memory_space=pltpu.VMEM),
        scratch_shapes=[
            pltpu.VMEM(slab_fields.shape, jnp.float32),
            pltpu.VMEM((1, 128), jnp.int32),
            pltpu.VMEM((1, 32), jnp.float32),
            pltpu.VMEM((1, 31), jnp.int32),
            pltpu.VMEM((3, 32, 128), jnp.float32),
            pltpu.VMEM((64, 64, 128), jnp.float32),
            pltpu.VMEM((1, 128), jnp.int32),
            pltpu.VMEM((2, 4, 288, 128), jnp.float32),
            pltpu.VMEM((2, 1088, 512), jnp.bfloat16),
            pltpu.SemaphoreType.DMA((64,)),
            pltpu.SemaphoreType.DMA,
            pltpu.SemaphoreType.DMA((2,)),
            pltpu.SemaphoreType.DMA((5,)),
        ],
        compiler_params=pltpu.CompilerParams(
            collective_id=0, has_side_effects=True, vmem_limit_bytes=53 * 1024 * 1024
        ),
    )(slab_fields, sample_index, thickness[None, :], level_cuts[None, :])


def solution(mesh):
    in_specs = (P(None, "lev", "hor"), P("hor", "lev"), P(), P())
    out_specs = P("hor", "lev")
    small = mesh.shape["lev"] == 2 and mesh.shape["hor"] == 16
    return jax.shard_map(
        on_slice if small else general_plan,
        mesh=mesh, in_specs=in_specs, out_specs=out_specs, check_vma=False,
    )
```

```python
import jax
import jax.numpy as jnp
from jax import lax
from jax.experimental import pallas as pl
from jax.experimental.pallas import tpu as pltpu
from jax.sharding import PartitionSpec as P

MESH = pl.DeviceIdType.MESH


def filter_weights(thickness, level_cuts):
    link = 1.0 - level_cuts.astype(jnp.float32)
    zero_one = jnp.zeros((1,), jnp.float32)
    lower_link = jnp.concatenate([zero_one, link])
    upper_link = jnp.concatenate([link, zero_one])
    lower_weight = jnp.concatenate([zero_one, thickness[:-1]]) * lower_link
    upper_weight = jnp.concatenate([thickness[1:], zero_one]) * upper_link
    return lower_weight, upper_weight


def vertical_filter(values, thickness, level_cuts):
    lower_weight, upper_weight = filter_weights(thickness, level_cuts)
    zero_row = jnp.zeros_like(values[:, :1, :])
    below = jnp.concatenate([zero_row, values[:, :-1, :]], axis=1)
    above = jnp.concatenate([values[:, 1:, :], zero_row], axis=1)
    numer = (
        2.0 * thickness[None, :, None] * values
        + lower_weight[None, :, None] * below
        + upper_weight[None, :, None] * above
    )
    denom = 2.0 * thickness + lower_weight + upper_weight
    return numer / denom[None, :, None]


def quadratic_features(smooth):
    count = smooth.shape[2]
    later = jnp.concatenate([smooth[2], smooth[3]], axis=0)
    earlier = jnp.concatenate([smooth[0], smooth[1]], axis=0)
    product = (later[:, None, :] * smooth[0][None, :, :]).reshape(-1, count)
    return jnp.concatenate([later, earlier, product], axis=0).astype(jnp.bfloat16)


def general_plan(slab_fields, sample_index, thickness, level_cuts):
    samp_count = sample_index.shape[1]
    lev_count = lax.axis_size("lev")
    hor_count = lax.axis_size("hor")
    all_lists = lax.all_gather(sample_index, "lev", axis=1, tiled=True)[0]
    group_cols = slab_fields.shape[2] // lev_count
    offsets = jnp.arange(all_lists.shape[0]) // samp_count * group_cols + all_lists
    chosen = jnp.take(slab_fields, offsets, axis=2)
    picked_cols = lax.all_to_all(chosen, "lev", split_axis=2, concat_axis=1, tiled=True)
    smooth = vertical_filter(picked_cols, thickness, level_cuts)
    feat_count = 4 * smooth.shape[1] + 2 * smooth.shape[1] * smooth.shape[1]
    col_count = feat_count // lev_count
    col_start = lax.axis_index("lev") * col_count
    features_bf = quadratic_features(smooth)
    block_features_bf = lax.all_gather(features_bf, "lev", axis=1, tiled=True)
    chosen_rows = lax.dynamic_slice_in_dim(block_features_bf, col_start, col_count, 0)
    column_block = lax.dot_general(
        block_features_bf, chosen_rows, (((1,), (1,)), ((), ())), preferred_element_type=jnp.float32
    )
    gram_block = lax.psum_scatter(column_block, "hor", scatter_dimension=0, tiled=True)
    count_all = samp_count * lev_count * hor_count
    return gram_block / count_all


def gram_kernel(
    slab_hbm, idx_hbm, thick_hbm, cuts_hbm, out_ref,
    slab_ref, idx_ref, thick_ref, cuts_ref, coef_ref, buf, other_idx,
    rows_ref, cols_ref, recv_sem, send_sem, idx_sem, local_sem,
):
    group_cols = slab_ref.shape[2] // 2
    x = lax.axis_index("lev")
    h = lax.axis_index("hor")
    z, y, c = h // 4, h // 2 % 2, h % 2

    def along_z(k):
        table = 228 + 145 * 256 + 122 * 256**2 + 15 * 256**3
        unit = (1 + 255 * (k % 2)) * (1 + 65535 * (k // 2)) * (1 + 3 * (z % 2)) * (1 + 15 * (z // 2))
        return table // unit % 4

    def place(zz, yy, cc):
        return zz * 4 + yy * 2 + cc

    def piece(xx, hh, g):
        return (xx * 16 + hh) * 2 + g

    x_mate = (1 - x, h)
    y_mate = (x, place(z, 1 - y, c))
    core_mate = (x, place(z, y, 1 - c))
    up_mate = (x, place((z + 1) % 4, y, c))
    down_mate = (x, place((z + 3) % 4, y, c))

    def send(p, target, sem=0):
        pltpu.make_async_remote_copy(
            src_ref=buf.at[p], dst_ref=buf.at[p], send_sem=send_sem.at[sem], recv_sem=recv_sem.at[p],
            device_id=target, device_id_type=MESH,
        ).start()

    def arrive(p):
        pltpu.make_async_copy(buf.at[p], buf.at[p], recv_sem.at[p]).wait()

    def load_group(g, sem):
        cols = pl.ds(pl.multiple_of(g * group_cols, group_cols), group_cols)
        return pltpu.make_async_copy(slab_hbm.at[:, :, cols], slab_ref.at[:, :, cols], sem)

    idx_load = pltpu.make_async_copy(idx_hbm, idx_ref, local_sem.at[0])
    thick_load = pltpu.make_async_copy(thick_hbm, thick_ref, local_sem.at[1])
    cuts_load = pltpu.make_async_copy(cuts_hbm, cuts_ref, local_sem.at[2])
    own_load = load_group(x, local_sem.at[3])
    other_load = load_group(1 - x, local_sem.at[4])
    for load in (idx_load, own_load, thick_load, cuts_load, other_load):
        load.start()

    barrier = pltpu.get_barrier_semaphore()
    for mate in [x_mate, y_mate, core_mate]:
        pl.semaphore_signal(barrier, inc=1, device_id=mate, device_id_type=MESH)

    @pl.when(z < 3)
    def _():
        pl.semaphore_signal(barrier, inc=1, device_id=up_mate, device_id_type=MESH)

    @pl.when(z > 0)
    def _():
        pl.semaphore_signal(barrier, inc=1, device_id=down_mate, device_id_type=MESH)

    out_ref[...] = jnp.zeros_like(out_ref)
    rows_ref[1] = jnp.zeros((4, 288, 128), jnp.float32)
    cols_ref[1] = jnp.zeros((1088, 512), jnp.bfloat16)
    pl.semaphore_wait(barrier, 5 - z // 3 - (3 - z) // 3)

    idx_copy = pltpu.make_async_remote_copy(
        src_ref=idx_hbm, dst_ref=other_idx, send_sem=idx_sem.at[0], recv_sem=idx_sem.at[1],
        device_id=x_mate, device_id_type=MESH,
    )
    idx_copy.start()

    def pick(g, idx_row):
        step = 512
        total = jnp.zeros((192, 128), jnp.float32)
        for t in range(group_cols // step):
            start = pl.multiple_of(g * group_cols + t * step, step)
            v = slab_ref[:, :, pl.ds(start, step)].reshape(64, step)
            hi = v.astype(jnp.bfloat16)
            rest = v - hi.astype(jnp.float32)
            mid = rest.astype(jnp.bfloat16)
            low = (rest - mid.astype(jnp.float32)).astype(jnp.bfloat16)
            parts = jnp.concatenate([hi, mid, low], axis=0)
            lane = lax.broadcasted_iota(jnp.int32, (step, 128), 0) + t * step
            hot = jnp.where(lane == idx_row, 1.0, 0.0).astype(jnp.bfloat16)
            total += jnp.dot(parts, hot, preferred_element_type=jnp.float32)
        p = piece(x, h, g)
        buf[p] = total[0:64] + total[64:128] + total[128:192]

        @pl.when(z < 3)
        def _():
            send(p, up_mate, 1)

        @pl.when(z > 0)
        def _():
            send(p, down_mate, 1)

        for mate in [x_mate, y_mate, core_mate]:
            send(p, mate)

    idx_load.wait()
    own_load.wait()
    pick(x, idx_ref[...])
    other_load.wait()
    idx_copy.wait_recv()
    pick(1 - x, other_idx[...])

    thick_load.wait()
    cuts_load.wait()

    def column(row, shift):
        shape = (32, row.shape[1])
        level = lax.broadcasted_iota(jnp.int32, shape, 0) + shift
        hit = level == lax.broadcasted_iota(jnp.int32, shape, 1)
        return jnp.sum(jnp.where(hit, row, 0.0), axis=1, keepdims=True)

    thick = thick_ref[...]
    link = 1.0 - cuts_ref[...].astype(jnp.float32)
    weights = [
        2.0 * column(thick, 0),
        column(thick, -1) * column(link, -1),
        column(thick, 1) * column(link, 0),
    ]
    denom = weights[0] + weights[1] + weights[2]
    for i in range(3):
        coef_ref[i] = jnp.broadcast_to(weights[i] / denom, (32, 128))

    def spread_z(k):
        zz = along_z(k)
        for i in range(2):
            p = piece(x, place(zz, y, c), (x + i) % 2)
            arrive(p)

            @pl.when((zz < z) & (z < 3))
            def _():
                send(p, up_mate, 1)

            @pl.when((zz > z) & (z > 0))
            def _():
                send(p, down_mate, 1)

            for mate in [x_mate, y_mate, core_mate]:
                send(p, mate)

    past_first = (h + 15) // 16
    first_row = (136 * h - 128) * past_first
    first_m = first_row // 32
    row_start = pl.multiple_of(past_first * (128 + first_row - 32 * first_m), 8)

    def features(hh, slot, half):
        for g in range(2):
            lanes = slice(half * 256 + g * 128, half * 256 + g * 128 + 128)
            q = half * 2 + g
            below_p, above_p = piece(0, hh, g), piece(1, hh, g)
            smooth = []
            for f in range(4):
                levels = slice(16 * f, 16 * f + 16)
                v = jnp.concatenate([buf[below_p, levels, :], buf[above_p, levels, :]], axis=0)
                smooth.append(
                    coef_ref[0] * v
                    + coef_ref[1] * pltpu.roll(v, 1, 0)
                    + coef_ref[2] * pltpu.roll(v, 31, 0)
                )
            base = smooth[0]
            direct = [smooth[2], smooth[3], smooth[0], smooth[1]]
            for b in range(4):
                rows_ref[slot, q, 32 * b:32 * b + 32, :] = direct[b]
            for i in range(5):
                m_row = rows_ref[slot, q, pl.ds(first_m + i, 1), :]
                rows_ref[slot, q, 128 + 32 * i:160 + 32 * i, :] = m_row * base
            chosen = jnp.where(x == 0, smooth[2], pltpu.roll(smooth[3], 30, 0))
            for b in range(34):
                if b < 2:
                    block = jnp.where(x == 0, direct[b], smooth[2][30 + b:31 + b] * base)
                elif b < 4:
                    block = jnp.where(x == 0, direct[b], smooth[3][b - 2:b - 1] * base)
                else:
                    block = chosen[b - 4:b - 3] * base
                cols_ref[slot, 32 * b:32 * b + 32, lanes] = block.astype(jnp.bfloat16)

    def add_product(slot):
        own = [rows_ref[slot, q, pl.ds(row_start, 136), :] for q in range(4)]
        out_ref[...] += lax.dot_general(
            jnp.concatenate(own, axis=1).astype(jnp.bfloat16), cols_ref[slot],
            (((1,), (1,)), ((), ())), preferred_element_type=jnp.float32,
        )

    def spread_near(k):
        zz = along_z(k)
        near, across = place(zz, y, c), place(zz, 1 - y, c)
        p = piece(1 - x, near, 1)
        arrive(p)
        send(p, y_mate)
        send(p, core_mate)
        p = piece(x, across, 0)
        arrive(p)
        send(p, x_mate)
        send(p, core_mate)
        for p in (piece(1 - x, near, 0), piece(x, across, 1)):
            arrive(p)
            send(p, core_mate)

    def spread_far(k):
        for g in range(2):
            p = piece(1 - x, place(along_z(k), 1 - y, c), g)
            arrive(p)
            send(p, core_mate)

    def step(u, carry):
        for part in range(4):
            j = 4 * u + part

            if part == 1:
                @pl.when(j == 1)
                def _():
                    spread_z(3)
                    spread_near(2)

            if part == 2:
                @pl.when(j == 2)
                def _():
                    spread_near(3)

            if part % 2 == 1:
                @pl.when((j >= 3) & (j <= 9))
                def _():
                    spread_far((j - 3) // 2)

            far = j // 8
            mate = (1 - far) * (j // 4 % 2) + far * (j // 2 % 2)
            k = (1 - far) * (j % 4) + far * (j % 8 // 4 * 2 + j % 2)
            hh = place(along_z(k), (y + far) % 2, (c + mate) % 2)

            @pl.when(mate == 1)
            def _():
                for xx in range(2):
                    for g in range(2):
                        arrive(piece(xx, hh, g))

            features(hh, part // 2, part % 2)
            if part % 2 == 1:
                add_product(1 - part // 2)
        return carry

    spread_z(1)
    spread_near(0)
    spread_z(2)
    spread_near(1)
    lax.fori_loop(0, 4, step, 0)
    add_product(1)
    out_ref[...] = out_ref[...] * (1.0 / 4096)

    def all_sent(count, sem):
        sent = buf.at[pl.ds(0, count)]
        pltpu.make_async_copy(sent, sent, send_sem.at[sem]).wait()

    all_sent(56, 0)
    middle = (z + 1) // 2 % 2

    @pl.when(middle == 1)
    def _():
        all_sent(10, 1)

    @pl.when(middle == 0)
    def _():
        all_sent(2, 1)

    idx_copy.wait_send()


def on_slice(slab_fields, sample_index, thickness, level_cuts):
    return pl.pallas_call(
        gram_kernel,
        out_shape=jax.ShapeDtypeStruct((136, 1088), jnp.float32),
        in_specs=[pl.BlockSpec(memory_space=pltpu.HBM)] * 4,
        out_specs=pl.BlockSpec(memory_space=pltpu.VMEM),
        scratch_shapes=[
            pltpu.VMEM(slab_fields.shape, jnp.float32),
            pltpu.VMEM((1, 128), jnp.int32),
            pltpu.VMEM((1, 32), jnp.float32),
            pltpu.VMEM((1, 31), jnp.int32),
            pltpu.VMEM((3, 32, 128), jnp.float32),
            pltpu.VMEM((64, 64, 128), jnp.float32),
            pltpu.VMEM((1, 128), jnp.int32),
            pltpu.VMEM((2, 4, 288, 128), jnp.float32),
            pltpu.VMEM((2, 1088, 512), jnp.bfloat16),
            pltpu.SemaphoreType.DMA((64,)),
            pltpu.SemaphoreType.DMA((2,)),
            pltpu.SemaphoreType.DMA((2,)),
            pltpu.SemaphoreType.DMA((5,)),
        ],
        compiler_params=pltpu.CompilerParams(
            collective_id=0, has_side_effects=True, vmem_limit_bytes=53 * 1024 * 1024
        ),
    )(slab_fields, sample_index, thickness[None, :], level_cuts[None, :])


def solution(mesh):
    in_specs = (P(None, "lev", "hor"), P("hor", "lev"), P(), P())
    out_specs = P("hor", "lev")
    small = mesh.shape["lev"] == 2 and mesh.shape["hor"] == 16
    return jax.shard_map(
        on_slice if small else general_plan,
        mesh=mesh, in_specs=in_specs, out_specs=out_specs, check_vma=False,
    )
```

```python
import jax
import jax.numpy as jnp
from jax import lax
from jax.experimental import pallas as pl
from jax.experimental.pallas import tpu as pltpu
from jax.sharding import PartitionSpec as P

MESH = pl.DeviceIdType.MESH


def filter_weights(thickness, level_cuts):
    link = 1.0 - level_cuts.astype(jnp.float32)
    zero_one = jnp.zeros((1,), jnp.float32)
    lower_link = jnp.concatenate([zero_one, link])
    upper_link = jnp.concatenate([link, zero_one])
    lower_weight = jnp.concatenate([zero_one, thickness[:-1]]) * lower_link
    upper_weight = jnp.concatenate([thickness[1:], zero_one]) * upper_link
    return lower_weight, upper_weight


def vertical_filter(values, thickness, level_cuts):
    lower_weight, upper_weight = filter_weights(thickness, level_cuts)
    zero_row = jnp.zeros_like(values[:, :1, :])
    below = jnp.concatenate([zero_row, values[:, :-1, :]], axis=1)
    above = jnp.concatenate([values[:, 1:, :], zero_row], axis=1)
    numer = (
        2.0 * thickness[None, :, None] * values
        + lower_weight[None, :, None] * below
        + upper_weight[None, :, None] * above
    )
    denom = 2.0 * thickness + lower_weight + upper_weight
    return numer / denom[None, :, None]


def quadratic_features(smooth):
    count = smooth.shape[2]
    later = jnp.concatenate([smooth[2], smooth[3]], axis=0)
    earlier = jnp.concatenate([smooth[0], smooth[1]], axis=0)
    product = (later[:, None, :] * smooth[0][None, :, :]).reshape(-1, count)
    return jnp.concatenate([later, earlier, product], axis=0).astype(jnp.bfloat16)


def general_plan(slab_fields, sample_index, thickness, level_cuts):
    samp_count = sample_index.shape[1]
    lev_count = lax.axis_size("lev")
    hor_count = lax.axis_size("hor")
    all_lists = lax.all_gather(sample_index, "lev", axis=1, tiled=True)[0]
    group_cols = slab_fields.shape[2] // lev_count
    offsets = jnp.arange(all_lists.shape[0]) // samp_count * group_cols + all_lists
    chosen = jnp.take(slab_fields, offsets, axis=2)
    picked_cols = lax.all_to_all(chosen, "lev", split_axis=2, concat_axis=1, tiled=True)
    smooth = vertical_filter(picked_cols, thickness, level_cuts)
    feat_count = 4 * smooth.shape[1] + 2 * smooth.shape[1] * smooth.shape[1]
    col_count = feat_count // lev_count
    col_start = lax.axis_index("lev") * col_count
    features_bf = quadratic_features(smooth)
    block_features_bf = lax.all_gather(features_bf, "lev", axis=1, tiled=True)
    chosen_rows = lax.dynamic_slice_in_dim(block_features_bf, col_start, col_count, 0)
    column_block = lax.dot_general(
        block_features_bf, chosen_rows, (((1,), (1,)), ((), ())), preferred_element_type=jnp.float32
    )
    gram_block = lax.psum_scatter(column_block, "hor", scatter_dimension=0, tiled=True)
    count_all = samp_count * lev_count * hor_count
    return gram_block / count_all


def gram_kernel(
    slab_hbm, idx_hbm, thick_hbm, cuts_hbm, out_ref,
    slab_ref, idx_ref, thick_ref, cuts_ref, coef_ref, buf, other_idx,
    rows_ref, cols_ref, recv_sem, send_sem, idx_sem, local_sem,
):
    group_cols = slab_ref.shape[2] // 2
    x = lax.axis_index("lev")
    h = lax.axis_index("hor")
    z, y, c = h // 4, h // 2 % 2, h % 2

    def along_z(k):
        table = 228 + 145 * 256 + 122 * 256**2 + 15 * 256**3
        unit = (1 + 255 * (k % 2)) * (1 + 65535 * (k // 2)) * (1 + 3 * (z % 2)) * (1 + 15 * (z // 2))
        return table // unit % 4

    def place(zz, yy, cc):
        return zz * 4 + yy * 2 + cc

    def pair(xx, hh):
        return xx * 16 + hh

    x_mate = (1 - x, h)
    y_mate = (x, place(z, 1 - y, c))
    core_mate = (x, place(z, y, 1 - c))
    z_mates = [(x, place(along_z(k), y, c)) for k in (1, 2, 3)]

    def send(p, target, g=None):
        part = buf.at[p] if g is None else buf.at[p, g]
        pltpu.make_async_remote_copy(
            src_ref=part, dst_ref=part, send_sem=send_sem, recv_sem=recv_sem.at[p],
            device_id=target, device_id_type=MESH,
        ).start()

    def arrive(p):
        pltpu.make_async_copy(buf.at[p], buf.at[p], recv_sem.at[p]).wait()

    def load_group(g, sem):
        cols = pl.ds(pl.multiple_of(g * group_cols, group_cols), group_cols)
        return pltpu.make_async_copy(slab_hbm.at[:, :, cols], slab_ref.at[:, :, cols], sem)

    idx_load = pltpu.make_async_copy(idx_hbm, idx_ref, local_sem.at[0])
    thick_load = pltpu.make_async_copy(thick_hbm, thick_ref, local_sem.at[1])
    cuts_load = pltpu.make_async_copy(cuts_hbm, cuts_ref, local_sem.at[2])
    own_load = load_group(x, local_sem.at[3])
    other_load = load_group(1 - x, local_sem.at[4])
    for load in (idx_load, own_load, thick_load, cuts_load, other_load):
        load.start()

    barrier = pltpu.get_barrier_semaphore()
    for mate in [x_mate, y_mate, core_mate] + z_mates:
        pl.semaphore_signal(barrier, inc=1, device_id=mate, device_id_type=MESH)
    out_ref[...] = jnp.zeros_like(out_ref)
    rows_ref[1] = jnp.zeros((4, 288, 128), jnp.float32)
    cols_ref[1] = jnp.zeros((1088, 512), jnp.bfloat16)
    pl.semaphore_wait(barrier, 6)

    idx_copy = pltpu.make_async_remote_copy(
        src_ref=idx_hbm, dst_ref=other_idx, send_sem=idx_sem.at[0], recv_sem=idx_sem.at[1],
        device_id=x_mate, device_id_type=MESH,
    )
    idx_copy.start()

    def pick(g, idx_row):
        step = 512
        total = jnp.zeros((192, 128), jnp.float32)
        for t in range(group_cols // step):
            start = pl.multiple_of(g * group_cols + t * step, step)
            v = slab_ref[:, :, pl.ds(start, step)].reshape(64, step)
            hi = v.astype(jnp.bfloat16)
            rest = v - hi.astype(jnp.float32)
            mid = rest.astype(jnp.bfloat16)
            low = (rest - mid.astype(jnp.float32)).astype(jnp.bfloat16)
            parts = jnp.concatenate([hi, mid, low], axis=0)
            lane = lax.broadcasted_iota(jnp.int32, (step, 128), 0) + t * step
            hot = jnp.where(lane == idx_row, 1.0, 0.0).astype(jnp.bfloat16)
            total += jnp.dot(parts, hot, preferred_element_type=jnp.float32)
        p = pair(x, h)
        buf[p, g] = total[0:64] + total[64:128] + total[128:192]
        for mate in z_mates + [x_mate, y_mate, core_mate]:
            send(p, mate, g)

    idx_load.wait()
    own_load.wait()
    pick(x, idx_ref[...])
    other_load.wait()
    idx_copy.wait_recv()
    pick(1 - x, other_idx[...])

    thick_load.wait()
    cuts_load.wait()

    def column(row, shift):
        shape = (32, row.shape[1])
        level = lax.broadcasted_iota(jnp.int32, shape, 0) + shift
        hit = level == lax.broadcasted_iota(jnp.int32, shape, 1)
        return jnp.sum(jnp.where(hit, row, 0.0), axis=1, keepdims=True)

    thick = thick_ref[...]
    link = 1.0 - cuts_ref[...].astype(jnp.float32)
    weights = [
        2.0 * column(thick, 0),
        column(thick, -1) * column(link, -1),
        column(thick, 1) * column(link, 0),
    ]
    denom = weights[0] + weights[1] + weights[2]
    for i in range(3):
        coef_ref[i] = jnp.broadcast_to(weights[i] / denom, (32, 128))

    def spread_z(k):
        p = pair(x, place(along_z(k), y, c))
        arrive(p)
        for mate in [x_mate, y_mate, core_mate]:
            send(p, mate)

    past_first = (h + 15) // 16
    first_row = (136 * h - 128) * past_first
    first_m = first_row // 32
    row_start = pl.multiple_of(past_first * (128 + first_row - 32 * first_m), 8)

    def features(hh, slot, half):
        for g in range(2):
            lanes = slice(half * 256 + g * 128, half * 256 + g * 128 + 128)
            q = half * 2 + g
            below_p, above_p = pair(0, hh), pair(1, hh)
            smooth = []
            for f in range(4):
                levels = slice(16 * f, 16 * f + 16)
                v = jnp.concatenate([buf[below_p, g, levels, :], buf[above_p, g, levels, :]], axis=0)
                smooth.append(
                    coef_ref[0] * v
                    + coef_ref[1] * pltpu.roll(v, 1, 0)
                    + coef_ref[2] * pltpu.roll(v, 31, 0)
                )
            base = smooth[0]
            direct = [smooth[2], smooth[3], smooth[0], smooth[1]]
            for b in range(4):
                rows_ref[slot, q, 32 * b:32 * b + 32, :] = direct[b]
            for i in range(5):
                m_row = rows_ref[slot, q, pl.ds(first_m + i, 1), :]
                rows_ref[slot, q, 128 + 32 * i:160 + 32 * i, :] = m_row * base
            chosen = jnp.where(x == 0, smooth[2], pltpu.roll(smooth[3], 30, 0))
            for b in range(34):
                if b < 2:
                    block = jnp.where(x == 0, direct[b], smooth[2][30 + b:31 + b] * base)
                elif b < 4:
                    block = jnp.where(x == 0, direct[b], smooth[3][b - 2:b - 1] * base)
                else:
                    block = chosen[b - 4:b - 3] * base
                cols_ref[slot, 32 * b:32 * b + 32, lanes] = block.astype(jnp.bfloat16)

    def add_product(slot):
        own = [rows_ref[slot, q, pl.ds(row_start, 136), :] for q in range(4)]
        out_ref[...] += lax.dot_general(
            jnp.concatenate(own, axis=1).astype(jnp.bfloat16), cols_ref[slot],
            (((1,), (1,)), ((), ())), preferred_element_type=jnp.float32,
        )

    def spread_near(k):
        zz = along_z(k)
        p = pair(1 - x, place(zz, y, c))
        arrive(p)
        send(p, y_mate, 1)
        send(p, core_mate)
        p = pair(x, place(zz, 1 - y, c))
        arrive(p)
        send(p, x_mate, 0)
        send(p, core_mate)

    def spread_far(k):
        p = pair(1 - x, place(along_z(k), 1 - y, c))
        arrive(p)
        send(p, core_mate)

    def step(u, carry):
        for part in range(4):
            j = 4 * u + part

            if part < 2:
                @pl.when(u == 0)
                def _():
                    spread_near(2 + part)

            if part % 2 == 1:
                @pl.when((j >= 3) & (j <= 9))
                def _():
                    spread_far((j - 3) // 2)

            far = j // 8
            mate = (1 - far) * (j // 4 % 2) + far * (j // 2 % 2)
            k = (1 - far) * (j % 4) + far * (j % 8 // 4 * 2 + j % 2)
            hh = place(along_z(k), (y + far) % 2, (c + mate) % 2)

            @pl.when(mate == 1)
            def _():
                for xx in range(2):
                    arrive(pair(xx, hh))

            features(hh, part // 2, part % 2)
            if part % 2 == 1:
                add_product(1 - part // 2)
        return carry

    spread_z(1)
    spread_near(0)
    spread_z(2)
    spread_near(1)
    spread_z(3)
    lax.fori_loop(0, 4, step, 0)
    add_product(1)
    out_ref[...] = out_ref[...] * (1.0 / 4096)
    sent = buf.at[pl.ds(0, 31)]
    pltpu.make_async_copy(sent, sent, send_sem).wait()
    idx_copy.wait_send()


def on_slice(slab_fields, sample_index, thickness, level_cuts):
    return pl.pallas_call(
        gram_kernel,
        out_shape=jax.ShapeDtypeStruct((136, 1088), jnp.float32),
        in_specs=[pl.BlockSpec(memory_space=pltpu.HBM)] * 4,
        out_specs=pl.BlockSpec(memory_space=pltpu.VMEM),
        scratch_shapes=[
            pltpu.VMEM(slab_fields.shape, jnp.float32),
            pltpu.VMEM((1, 128), jnp.int32),
            pltpu.VMEM((1, 32), jnp.float32),
            pltpu.VMEM((1, 31), jnp.int32),
            pltpu.VMEM((3, 32, 128), jnp.float32),
            pltpu.VMEM((32, 2, 64, 128), jnp.float32),
            pltpu.VMEM((1, 128), jnp.int32),
            pltpu.VMEM((2, 4, 288, 128), jnp.float32),
            pltpu.VMEM((2, 1088, 512), jnp.bfloat16),
            pltpu.SemaphoreType.DMA((32,)),
            pltpu.SemaphoreType.DMA,
            pltpu.SemaphoreType.DMA((2,)),
            pltpu.SemaphoreType.DMA((5,)),
        ],
        compiler_params=pltpu.CompilerParams(
            collective_id=0, has_side_effects=True, vmem_limit_bytes=53 * 1024 * 1024
        ),
    )(slab_fields, sample_index, thickness[None, :], level_cuts[None, :])


def solution(mesh):
    in_specs = (P(None, "lev", "hor"), P("hor", "lev"), P(), P())
    out_specs = P("hor", "lev")
    small = mesh.shape["lev"] == 2 and mesh.shape["hor"] == 16
    return jax.shard_map(
        on_slice if small else general_plan,
        mesh=mesh, in_specs=in_specs, out_specs=out_specs, check_vma=False,
    )
```

```python
import jax
import jax.numpy as jnp
from jax import lax
from jax.experimental import pallas as pl
from jax.experimental.pallas import tpu as pltpu
from jax.sharding import PartitionSpec as P

MESH = pl.DeviceIdType.MESH


def filter_weights(thickness, level_cuts):
    link = 1.0 - level_cuts.astype(jnp.float32)
    zero_one = jnp.zeros((1,), jnp.float32)
    lower_link = jnp.concatenate([zero_one, link])
    upper_link = jnp.concatenate([link, zero_one])
    lower_weight = jnp.concatenate([zero_one, thickness[:-1]]) * lower_link
    upper_weight = jnp.concatenate([thickness[1:], zero_one]) * upper_link
    return lower_weight, upper_weight


def vertical_filter(values, thickness, level_cuts):
    lower_weight, upper_weight = filter_weights(thickness, level_cuts)
    zero_row = jnp.zeros_like(values[:, :1, :])
    below = jnp.concatenate([zero_row, values[:, :-1, :]], axis=1)
    above = jnp.concatenate([values[:, 1:, :], zero_row], axis=1)
    numer = (
        2.0 * thickness[None, :, None] * values
        + lower_weight[None, :, None] * below
        + upper_weight[None, :, None] * above
    )
    denom = 2.0 * thickness + lower_weight + upper_weight
    return numer / denom[None, :, None]


def quadratic_features(smooth):
    count = smooth.shape[2]
    later = jnp.concatenate([smooth[2], smooth[3]], axis=0)
    earlier = jnp.concatenate([smooth[0], smooth[1]], axis=0)
    product = (later[:, None, :] * smooth[0][None, :, :]).reshape(-1, count)
    return jnp.concatenate([later, earlier, product], axis=0).astype(jnp.bfloat16)


def general_plan(slab_fields, sample_index, thickness, level_cuts):
    samp_count = sample_index.shape[1]
    lev_count = lax.axis_size("lev")
    hor_count = lax.axis_size("hor")
    all_lists = lax.all_gather(sample_index, "lev", axis=1, tiled=True)[0]
    group_cols = slab_fields.shape[2] // lev_count
    offsets = jnp.arange(all_lists.shape[0]) // samp_count * group_cols + all_lists
    chosen = jnp.take(slab_fields, offsets, axis=2)
    picked_cols = lax.all_to_all(chosen, "lev", split_axis=2, concat_axis=1, tiled=True)
    smooth = vertical_filter(picked_cols, thickness, level_cuts)
    feat_count = 4 * smooth.shape[1] + 2 * smooth.shape[1] * smooth.shape[1]
    col_count = feat_count // lev_count
    col_start = lax.axis_index("lev") * col_count
    features_bf = quadratic_features(smooth)
    block_features_bf = lax.all_gather(features_bf, "lev", axis=1, tiled=True)
    chosen_rows = lax.dynamic_slice_in_dim(block_features_bf, col_start, col_count, 0)
    column_block = lax.dot_general(
        block_features_bf, chosen_rows, (((1,), (1,)), ((), ())), preferred_element_type=jnp.float32
    )
    gram_block = lax.psum_scatter(column_block, "hor", scatter_dimension=0, tiled=True)
    count_all = samp_count * lev_count * hor_count
    return gram_block / count_all


def gram_kernel(
    slab_hbm, idx_hbm, thick_hbm, cuts_hbm, out_ref,
    slab_ref, idx_ref, thick_ref, cuts_ref, coef_ref, buf, other_idx,
    rows_ref, cols_ref, recv_sem, send_sem, idx_sem, local_sem,
):
    group_cols = slab_ref.shape[2] // 2
    x = lax.axis_index("lev")
    h = lax.axis_index("hor")
    z, y, c = h // 4, h // 2 % 2, h % 2

    def along_z(k):
        return (z // 2 + k // 2) % 2 * 2 + (z + k) % 2

    def place(zz, yy, cc):
        return zz * 4 + yy * 2 + cc

    def piece(xx, hh, g):
        return (xx * 16 + hh) * 2 + g

    x_mate = (1 - x, h)
    y_mate = (x, place(z, 1 - y, c))
    core_mate = (x, place(z, y, 1 - c))
    z_mates = [(x, place(along_z(k), y, c)) for k in (1, 2, 3)]

    def send(p, target):
        pltpu.make_async_remote_copy(
            src_ref=buf.at[p], dst_ref=buf.at[p], send_sem=send_sem, recv_sem=recv_sem.at[p],
            device_id=target, device_id_type=MESH,
        ).start()

    def arrive(p):
        pltpu.make_async_copy(buf.at[p], buf.at[p], recv_sem.at[p]).wait()

    def load_group(g, sem):
        cols = pl.ds(pl.multiple_of(g * group_cols, group_cols), group_cols)
        return pltpu.make_async_copy(slab_hbm.at[:, :, cols], slab_ref.at[:, :, cols], sem)

    idx_load = pltpu.make_async_copy(idx_hbm, idx_ref, local_sem.at[0])
    thick_load = pltpu.make_async_copy(thick_hbm, thick_ref, local_sem.at[1])
    cuts_load = pltpu.make_async_copy(cuts_hbm, cuts_ref, local_sem.at[2])
    own_load = load_group(x, local_sem.at[3])
    other_load = load_group(1 - x, local_sem.at[4])
    for load in (idx_load, own_load, thick_load, cuts_load, other_load):
        load.start()

    barrier = pltpu.get_barrier_semaphore()
    for mate in [x_mate, y_mate, core_mate] + z_mates:
        pl.semaphore_signal(barrier, inc=1, device_id=mate, device_id_type=MESH)
    out_ref[...] = jnp.zeros_like(out_ref)
    rows_ref[1] = jnp.zeros((4, 288, 128), jnp.float32)
    cols_ref[1] = jnp.zeros((1088, 512), jnp.bfloat16)
    pl.semaphore_wait(barrier, 6)

    idx_copy = pltpu.make_async_remote_copy(
        src_ref=idx_hbm, dst_ref=other_idx, send_sem=idx_sem.at[0], recv_sem=idx_sem.at[1],
        device_id=x_mate, device_id_type=MESH,
    )
    idx_copy.start()

    def pick(g, idx_row):
        step = 512
        total = jnp.zeros((192, 128), jnp.float32)
        for t in range(group_cols // step):
            start = pl.multiple_of(g * group_cols + t * step, step)
            v = slab_ref[:, :, pl.ds(start, step)].reshape(64, step)
            hi = v.astype(jnp.bfloat16)
            rest = v - hi.astype(jnp.float32)
            mid = rest.astype(jnp.bfloat16)
            low = (rest - mid.astype(jnp.float32)).astype(jnp.bfloat16)
            parts = jnp.concatenate([hi, mid, low], axis=0)
            lane = lax.broadcasted_iota(jnp.int32, (step, 128), 0) + t * step
            hot = jnp.where(lane == idx_row, 1.0, 0.0).astype(jnp.bfloat16)
            total += jnp.dot(parts, hot, preferred_element_type=jnp.float32)
        p = piece(x, h, g)
        buf[p] = total[0:64] + total[64:128] + total[128:192]
        for mate in [x_mate, y_mate] + z_mates + [core_mate]:
            send(p, mate)

    idx_load.wait()
    own_load.wait()
    pick(x, idx_ref[...])
    other_load.wait()
    idx_copy.wait_recv()
    pick(1 - x, other_idx[...])

    thick_load.wait()
    cuts_load.wait()

    def column(row, shift):
        shape = (32, row.shape[1])
        level = lax.broadcasted_iota(jnp.int32, shape, 0) + shift
        hit = level == lax.broadcasted_iota(jnp.int32, shape, 1)
        return jnp.sum(jnp.where(hit, row, 0.0), axis=1, keepdims=True)

    thick = thick_ref[...]
    link = 1.0 - cuts_ref[...].astype(jnp.float32)
    weights = [
        2.0 * column(thick, 0),
        column(thick, -1) * column(link, -1),
        column(thick, 1) * column(link, 0),
    ]
    denom = weights[0] + weights[1] + weights[2]
    for i in range(3):
        coef_ref[i] = jnp.broadcast_to(weights[i] / denom, (32, 128))

    def forward_z(i, carry):
        g = (x + i) % 2
        p = piece(x, place(along_z(1 + i // 2), y, c), g)
        arrive(p)
        for mate in [x_mate, y_mate, core_mate]:
            send(p, mate)
        return carry

    lax.fori_loop(0, 6, forward_z, 0)

    past_first = (h + 15) // 16
    first_row = (136 * h - 128) * past_first
    first_m = first_row // 32
    row_start = pl.multiple_of(past_first * (128 + first_row - 32 * first_m), 8)

    def features(hh, slot, half):
        for g in range(2):
            lanes = slice(half * 256 + g * 128, half * 256 + g * 128 + 128)
            q = half * 2 + g
            below_p, above_p = piece(0, hh, g), piece(1, hh, g)
            smooth = []
            for f in range(4):
                levels = slice(16 * f, 16 * f + 16)
                v = jnp.concatenate([buf[below_p, levels, :], buf[above_p, levels, :]], axis=0)
                smooth.append(
                    coef_ref[0] * v
                    + coef_ref[1] * pltpu.roll(v, 1, 0)
                    + coef_ref[2] * pltpu.roll(v, 31, 0)
                )
            base = smooth[0]
            direct = [smooth[2], smooth[3], smooth[0], smooth[1]]
            for b in range(4):
                rows_ref[slot, q, 32 * b:32 * b + 32, :] = direct[b]
            for i in range(5):
                m_row = rows_ref[slot, q, pl.ds(first_m + i, 1), :]
                rows_ref[slot, q, 128 + 32 * i:160 + 32 * i, :] = m_row * base
            chosen = jnp.where(x == 0, smooth[2], pltpu.roll(smooth[3], 30, 0))
            for b in range(34):
                if b < 2:
                    block = jnp.where(x == 0, direct[b], smooth[2][30 + b:31 + b] * base)
                elif b < 4:
                    block = jnp.where(x == 0, direct[b], smooth[3][b - 2:b - 1] * base)
                else:
                    block = chosen[b - 4:b - 3] * base
                cols_ref[slot, 32 * b:32 * b + 32, lanes] = block.astype(jnp.bfloat16)

    def add_product(slot):
        own = [rows_ref[slot, q, pl.ds(row_start, 136), :] for q in range(4)]
        out_ref[...] += lax.dot_general(
            jnp.concatenate(own, axis=1).astype(jnp.bfloat16), cols_ref[slot],
            (((1,), (1,)), ((), ())), preferred_element_type=jnp.float32,
        )

    def spread_near(k):
        zz = along_z(k)
        near, across = place(zz, y, c), place(zz, 1 - y, c)
        p = piece(1 - x, near, 1)
        arrive(p)
        send(p, y_mate)
        send(p, core_mate)
        p = piece(x, across, 0)
        arrive(p)
        send(p, x_mate)
        send(p, core_mate)
        for p in (piece(1 - x, near, 0), piece(x, across, 1)):
            arrive(p)
            send(p, core_mate)

    def spread_far(k):
        for g in range(2):
            p = piece(1 - x, place(along_z(k), 1 - y, c), g)
            arrive(p)
            send(p, core_mate)

    def step(u, carry):
        for part in range(4):
            j = 4 * u + part

            @pl.when(u == 0)
            def _():
                spread_near(j)

            far = u // 2
            k_of = (part, part, (0, 1, 0, 2)[part], (1, 3, 2, 3)[part])
            mate_of = (0, 1, (0, 0, 1, 0)[part], (1, 0, 1, 1)[part])
            unit = (1 + 3 * (u % 2)) * (1 + 15 * (u // 2))
            k = sum(v * 4**i for i, v in enumerate(k_of)) // unit % 4
            mate = sum(v * 4**i for i, v in enumerate(mate_of)) // unit % 4

            @pl.when((far == 1) & (mate == 0))
            def _():
                spread_far(k)

            hh = place(along_z(k), (y + far) % 2, (c + mate) % 2)

            @pl.when(mate == 1)
            def _():
                for xx in range(2):
                    for g in range(2):
                        arrive(piece(xx, hh, g))

            features(hh, part // 2, part % 2)
            if part % 2 == 1:
                add_product(1 - part // 2)
        return carry

    lax.fori_loop(0, 4, step, 0)
    add_product(1)
    out_ref[...] = out_ref[...] * (1.0 / 4096)
    sent = buf.at[pl.ds(0, 62)]
    pltpu.make_async_copy(sent, sent, send_sem).wait()
    idx_copy.wait_send()


def on_slice(slab_fields, sample_index, thickness, level_cuts):
    return pl.pallas_call(
        gram_kernel,
        out_shape=jax.ShapeDtypeStruct((136, 1088), jnp.float32),
        in_specs=[pl.BlockSpec(memory_space=pltpu.HBM)] * 4,
        out_specs=pl.BlockSpec(memory_space=pltpu.VMEM),
        scratch_shapes=[
            pltpu.VMEM(slab_fields.shape, jnp.float32),
            pltpu.VMEM((1, 128), jnp.int32),
            pltpu.VMEM((1, 32), jnp.float32),
            pltpu.VMEM((1, 31), jnp.int32),
            pltpu.VMEM((3, 32, 128), jnp.float32),
            pltpu.VMEM((64, 64, 128), jnp.float32),
            pltpu.VMEM((1, 128), jnp.int32),
            pltpu.VMEM((2, 4, 288, 128), jnp.float32),
            pltpu.VMEM((2, 1088, 512), jnp.bfloat16),
            pltpu.SemaphoreType.DMA((64,)),
            pltpu.SemaphoreType.DMA,
            pltpu.SemaphoreType.DMA((2,)),
            pltpu.SemaphoreType.DMA((5,)),
        ],
        compiler_params=pltpu.CompilerParams(
            collective_id=0, has_side_effects=True, vmem_limit_bytes=53 * 1024 * 1024
        ),
    )(slab_fields, sample_index, thickness[None, :], level_cuts[None, :])


def solution(mesh):
    in_specs = (P(None, "lev", "hor"), P("hor", "lev"), P(), P())
    out_specs = P("hor", "lev")
    small = mesh.shape["lev"] == 2 and mesh.shape["hor"] == 16
    return jax.shard_map(
        on_slice if small else general_plan,
        mesh=mesh, in_specs=in_specs, out_specs=out_specs, check_vma=False,
    )
```

```python
import jax
import jax.numpy as jnp
from jax import lax
from jax.experimental import pallas as pl
from jax.experimental.pallas import tpu as pltpu
from jax.sharding import PartitionSpec as P

MESH = pl.DeviceIdType.MESH


def filter_weights(thickness, level_cuts):
    link = 1.0 - level_cuts.astype(jnp.float32)
    zero_one = jnp.zeros((1,), jnp.float32)
    lower_link = jnp.concatenate([zero_one, link])
    upper_link = jnp.concatenate([link, zero_one])
    lower_weight = jnp.concatenate([zero_one, thickness[:-1]]) * lower_link
    upper_weight = jnp.concatenate([thickness[1:], zero_one]) * upper_link
    return lower_weight, upper_weight


def vertical_filter(values, thickness, level_cuts):
    lower_weight, upper_weight = filter_weights(thickness, level_cuts)
    zero_row = jnp.zeros_like(values[:, :1, :])
    below = jnp.concatenate([zero_row, values[:, :-1, :]], axis=1)
    above = jnp.concatenate([values[:, 1:, :], zero_row], axis=1)
    numer = (
        2.0 * thickness[None, :, None] * values
        + lower_weight[None, :, None] * below
        + upper_weight[None, :, None] * above
    )
    denom = 2.0 * thickness + lower_weight + upper_weight
    return numer / denom[None, :, None]


def quadratic_features(smooth):
    count = smooth.shape[2]
    later = jnp.concatenate([smooth[2], smooth[3]], axis=0)
    earlier = jnp.concatenate([smooth[0], smooth[1]], axis=0)
    product = (later[:, None, :] * smooth[0][None, :, :]).reshape(-1, count)
    return jnp.concatenate([later, earlier, product], axis=0).astype(jnp.bfloat16)


def general_plan(slab_fields, sample_index, thickness, level_cuts):
    samp_count = sample_index.shape[1]
    lev_count = lax.axis_size("lev")
    hor_count = lax.axis_size("hor")
    all_lists = lax.all_gather(sample_index, "lev", axis=1, tiled=True)[0]
    group_cols = slab_fields.shape[2] // lev_count
    offsets = jnp.arange(all_lists.shape[0]) // samp_count * group_cols + all_lists
    chosen = jnp.take(slab_fields, offsets, axis=2)
    picked_cols = lax.all_to_all(chosen, "lev", split_axis=2, concat_axis=1, tiled=True)
    smooth = vertical_filter(picked_cols, thickness, level_cuts)
    feat_count = 4 * smooth.shape[1] + 2 * smooth.shape[1] * smooth.shape[1]
    col_count = feat_count // lev_count
    col_start = lax.axis_index("lev") * col_count
    features_bf = quadratic_features(smooth)
    block_features_bf = lax.all_gather(features_bf, "lev", axis=1, tiled=True)
    chosen_rows = lax.dynamic_slice_in_dim(block_features_bf, col_start, col_count, 0)
    column_block = lax.dot_general(
        block_features_bf, chosen_rows, (((1,), (1,)), ((), ())), preferred_element_type=jnp.float32
    )
    gram_block = lax.psum_scatter(column_block, "hor", scatter_dimension=0, tiled=True)
    count_all = samp_count * lev_count * hor_count
    return gram_block / count_all


def gram_kernel(
    slab_hbm, idx_hbm, thick_hbm, cuts_hbm, out_ref,
    slab_ref, idx_ref, thick_ref, cuts_ref, coef_ref, buf, other_idx,
    rows_ref, cols_ref, recv_sem, send_sem, idx_sem, local_sem,
):
    group_cols = slab_ref.shape[2] // 2
    x = lax.axis_index("lev")
    h = lax.axis_index("hor")
    z, y, c = h // 4, h // 2 % 2, h % 2

    def along_z(k):
        return (z // 2 + k // 2) % 2 * 2 + (z + k) % 2

    def place(zz, yy, cc):
        return zz * 4 + yy * 2 + cc

    def piece(xx, hh, g):
        return (xx * 16 + hh) * 2 + g

    x_mate = (1 - x, h)
    y_mate = (x, place(z, 1 - y, c))
    core_mate = (x, place(z, y, 1 - c))
    z_mates = [(x, place(along_z(k), y, c)) for k in (1, 2, 3)]

    def send(p, target):
        pltpu.make_async_remote_copy(
            src_ref=buf.at[p], dst_ref=buf.at[p], send_sem=send_sem, recv_sem=recv_sem.at[p],
            device_id=target, device_id_type=MESH,
        ).start()

    def arrive(p):
        pltpu.make_async_copy(buf.at[p], buf.at[p], recv_sem.at[p]).wait()

    def load_group(g, sem):
        cols = pl.ds(pl.multiple_of(g * group_cols, group_cols), group_cols)
        return pltpu.make_async_copy(slab_hbm.at[:, :, cols], slab_ref.at[:, :, cols], sem)

    idx_load = pltpu.make_async_copy(idx_hbm, idx_ref, local_sem.at[0])
    thick_load = pltpu.make_async_copy(thick_hbm, thick_ref, local_sem.at[1])
    cuts_load = pltpu.make_async_copy(cuts_hbm, cuts_ref, local_sem.at[2])
    own_load = load_group(x, local_sem.at[3])
    other_load = load_group(1 - x, local_sem.at[4])
    for load in (idx_load, own_load, thick_load, cuts_load, other_load):
        load.start()

    barrier = pltpu.get_barrier_semaphore()
    for mate in [x_mate, y_mate, core_mate] + z_mates:
        pl.semaphore_signal(barrier, inc=1, device_id=mate, device_id_type=MESH)
    out_ref[...] = jnp.zeros_like(out_ref)
    rows_ref[1] = jnp.zeros((4, 288, 128), jnp.float32)
    cols_ref[1] = jnp.zeros((1088, 512), jnp.bfloat16)
    pl.semaphore_wait(barrier, 6)

    idx_copy = pltpu.make_async_remote_copy(
        src_ref=idx_hbm, dst_ref=other_idx, send_sem=idx_sem.at[0], recv_sem=idx_sem.at[1],
        device_id=x_mate, device_id_type=MESH,
    )
    idx_copy.start()

    def pick(g, idx_row):
        step = 512
        total = jnp.zeros((192, 128), jnp.float32)
        for t in range(group_cols // step):
            start = pl.multiple_of(g * group_cols + t * step, step)
            v = slab_ref[:, :, pl.ds(start, step)].reshape(64, step)
            hi = v.astype(jnp.bfloat16)
            rest = v - hi.astype(jnp.float32)
            mid = rest.astype(jnp.bfloat16)
            low = (rest - mid.astype(jnp.float32)).astype(jnp.bfloat16)
            parts = jnp.concatenate([hi, mid, low], axis=0)
            lane = lax.broadcasted_iota(jnp.int32, (step, 128), 0) + t * step
            hot = jnp.where(lane == idx_row, 1.0, 0.0).astype(jnp.bfloat16)
            total += jnp.dot(parts, hot, preferred_element_type=jnp.float32)
        p = piece(x, h, g)
        buf[p] = total[0:64] + total[64:128] + total[128:192]
        for mate in [x_mate, y_mate] + z_mates + [core_mate]:
            send(p, mate)

    idx_load.wait()
    own_load.wait()
    pick(x, idx_ref[...])
    thick_load.wait()
    cuts_load.wait()

    def column(row, shift):
        shape = (32, row.shape[1])
        level = lax.broadcasted_iota(jnp.int32, shape, 0) + shift
        hit = level == lax.broadcasted_iota(jnp.int32, shape, 1)
        return jnp.sum(jnp.where(hit, row, 0.0), axis=1, keepdims=True)

    thick = thick_ref[...]
    link = 1.0 - cuts_ref[...].astype(jnp.float32)
    weights = [
        2.0 * column(thick, 0),
        column(thick, -1) * column(link, -1),
        column(thick, 1) * column(link, 0),
    ]
    denom = weights[0] + weights[1] + weights[2]
    for i in range(3):
        coef_ref[i] = jnp.broadcast_to(weights[i] / denom, (32, 128))

    other_load.wait()
    idx_copy.wait_recv()
    pick(1 - x, other_idx[...])

    def forward_z(i, carry):
        g = (x + i) % 2
        p = piece(x, place(along_z(1 + i // 2), y, c), g)
        arrive(p)
        for mate in [x_mate, y_mate, core_mate]:
            send(p, mate)
        return carry

    lax.fori_loop(0, 6, forward_z, 0)

    past_first = (h + 15) // 16
    first_row = (136 * h - 128) * past_first
    first_m = first_row // 32
    row_start = pl.multiple_of(past_first * (128 + first_row - 32 * first_m), 8)

    def features(hh, slot, half):
        for g in range(2):
            lanes = slice(half * 256 + g * 128, half * 256 + g * 128 + 128)
            q = half * 2 + g
            below_p, above_p = piece(0, hh, g), piece(1, hh, g)
            smooth = []
            for f in range(4):
                levels = slice(16 * f, 16 * f + 16)
                v = jnp.concatenate([buf[below_p, levels, :], buf[above_p, levels, :]], axis=0)
                smooth.append(
                    coef_ref[0] * v
                    + coef_ref[1] * pltpu.roll(v, 1, 0)
                    + coef_ref[2] * pltpu.roll(v, 31, 0)
                )
            base = smooth[0]
            direct = [smooth[2], smooth[3], smooth[0], smooth[1]]
            for b in range(4):
                rows_ref[slot, q, 32 * b:32 * b + 32, :] = direct[b]
            for i in range(5):
                m_row = rows_ref[slot, q, pl.ds(first_m + i, 1), :]
                rows_ref[slot, q, 128 + 32 * i:160 + 32 * i, :] = m_row * base
            chosen = jnp.where(x == 0, smooth[2], pltpu.roll(smooth[3], 30, 0))
            for b in range(34):
                if b < 2:
                    block = jnp.where(x == 0, direct[b], smooth[2][30 + b:31 + b] * base)
                elif b < 4:
                    block = jnp.where(x == 0, direct[b], smooth[3][b - 2:b - 1] * base)
                else:
                    block = chosen[b - 4:b - 3] * base
                cols_ref[slot, 32 * b:32 * b + 32, lanes] = block.astype(jnp.bfloat16)

    def add_product(slot):
        own = [rows_ref[slot, q, pl.ds(row_start, 136), :] for q in range(4)]
        out_ref[...] += lax.dot_general(
            jnp.concatenate(own, axis=1).astype(jnp.bfloat16), cols_ref[slot],
            (((1,), (1,)), ((), ())), preferred_element_type=jnp.float32,
        )

    def spread_near(k):
        zz = along_z(k)
        near, across = place(zz, y, c), place(zz, 1 - y, c)
        p = piece(1 - x, near, 1)
        arrive(p)
        send(p, y_mate)
        send(p, core_mate)
        p = piece(x, across, 0)
        arrive(p)
        send(p, x_mate)
        send(p, core_mate)
        for p in (piece(1 - x, near, 0), piece(x, across, 1)):
            arrive(p)
            send(p, core_mate)

    def spread_far(k):
        for g in range(2):
            p = piece(1 - x, place(along_z(k), 1 - y, c), g)
            arrive(p)
            send(p, core_mate)

    def step(u, carry):
        for part in range(4):
            j = 4 * u + part

            @pl.when(u == 0)
            def _():
                spread_near(j)

            far = u // 2
            k_of = (part, part, (0, 1, 0, 2)[part], (1, 3, 2, 3)[part])
            mate_of = (0, 1, (0, 0, 1, 0)[part], (1, 0, 1, 1)[part])
            unit = (1 + 3 * (u % 2)) * (1 + 15 * (u // 2))
            k = sum(v * 4**i for i, v in enumerate(k_of)) // unit % 4
            mate = sum(v * 4**i for i, v in enumerate(mate_of)) // unit % 4

            @pl.when((far == 1) & (mate == 0))
            def _():
                spread_far(k)

            hh = place(along_z(k), (y + far) % 2, (c + mate) % 2)

            @pl.when(mate == 1)
            def _():
                for xx in range(2):
                    for g in range(2):
                        arrive(piece(xx, hh, g))

            features(hh, part // 2, part % 2)
            if part % 2 == 1:
                add_product(1 - part // 2)
        return carry

    lax.fori_loop(0, 4, step, 0)
    add_product(1)
    out_ref[...] = out_ref[...] * (1.0 / 4096)
    sent = buf.at[pl.ds(0, 62)]
    pltpu.make_async_copy(sent, sent, send_sem).wait()
    idx_copy.wait_send()


def on_slice(slab_fields, sample_index, thickness, level_cuts):
    return pl.pallas_call(
        gram_kernel,
        out_shape=jax.ShapeDtypeStruct((136, 1088), jnp.float32),
        in_specs=[pl.BlockSpec(memory_space=pltpu.HBM)] * 4,
        out_specs=pl.BlockSpec(memory_space=pltpu.VMEM),
        scratch_shapes=[
            pltpu.VMEM(slab_fields.shape, jnp.float32),
            pltpu.VMEM((1, 128), jnp.int32),
            pltpu.VMEM((1, 32), jnp.float32),
            pltpu.VMEM((1, 31), jnp.int32),
            pltpu.VMEM((3, 32, 128), jnp.float32),
            pltpu.VMEM((64, 64, 128), jnp.float32),
            pltpu.VMEM((1, 128), jnp.int32),
            pltpu.VMEM((2, 4, 288, 128), jnp.float32),
            pltpu.VMEM((2, 1088, 512), jnp.bfloat16),
            pltpu.SemaphoreType.DMA((64,)),
            pltpu.SemaphoreType.DMA,
            pltpu.SemaphoreType.DMA((2,)),
            pltpu.SemaphoreType.DMA((5,)),
        ],
        compiler_params=pltpu.CompilerParams(
            collective_id=0, has_side_effects=True, vmem_limit_bytes=53 * 1024 * 1024
        ),
    )(slab_fields, sample_index, thickness[None, :], level_cuts[None, :])


def solution(mesh):
    in_specs = (P(None, "lev", "hor"), P("hor", "lev"), P(), P())
    out_specs = P("hor", "lev")
    small = mesh.shape["lev"] == 2 and mesh.shape["hor"] == 16
    return jax.shard_map(
        on_slice if small else general_plan,
        mesh=mesh, in_specs=in_specs, out_specs=out_specs, check_vma=False,
    )
```
